512 devices in a mesh: tm: 8 (over x, z_lo), space: 64 (over z_hi, y, core).
Axes of the slice: x: 4, y: 8, z: 8 (z_hi: 4, z_lo: 2; z = z_hi * 2 + z_lo), core: 2. Of those that a mesh axis runs over, the one named last changes fastest.
Arguments:
- model_departure: float32 [8, 1024, 8, 384], P('tm', 'space'), may hold values from -24 to 24, as said below
- obs_departure: float32 [8, 131072], P('tm', 'space'), may hold values from -6 to 6
- obs_variance: float32 [8, 131072], P('tm', 'space'), may hold values from 0.5 to 2
- obs_weight: float32 [8, 8, 131072], P('tm', None, 'space'), may hold values from -2 to 2
- obs_index: int32 [8, 131072], P('tm', 'space'), may hold values from 0 to 6143
- obs_count: int32 [8, 64], P('tm', 'space'), may hold values from 1024 to 2048, as said below
- courant: float32 [8, 1024, 8, 384], P('tm', 'space'), may hold values from 0.3 to 0.95
- diffusion: float32 [8, 8, 384], P('tm'), may hold values from 0.02 to 0.45
- vertical_mix: float32 [8, 8, 8], P('tm'), may hold values from -0.75 to 0.75
- error_variance: float32 [8, 1024, 3072], P('tm', None, 'space'), may hold values from 0.2 to 2
Outputs:
- multiplier: float32 [8, 1024, 8, 384], P('tm', 'space')
- obs_multiplier: float32 [8, 131072], P('tm', 'space')
- increment: float32 [8, 1024, 8, 384], P('tm', 'space')
The draws below stay inside these ranges and needn't reach their ends.
Inputs may be any that keep to these rules, and one draw needn't show every extreme that they name: `model_departure`: smooth trends and level-latitude scales times random entries; entries lie within -24 to 24. `obs_count`: some tile of some sub-window holds exactly 2048 live slots and some exactly 1024.
All inputs are finite; a program needn't handle non-finite values.
Results may differ from the reference program's by a relative error of at most 0.0001.
Values sent between devices are 32-bit elements; how exact they have to be, the bound alone decides.
A program may use at most 64 MiB of HBM per device.

```python
import math
import jax
import jax.numpy as jnp
from jax import lax

LON_DEV = 16
LAT = 384
LEV = 8
OBS_DEV = 2048
STEPS = 4
ITERS = 2
HAAR = 6
WINDOWS = 8
TILES = 64
NLON = 1024


def draw_model_departure(key, part):
    key = jax.random.fold_in(key, 17)
    random_key, scale_key = jax.random.split(key)
    full_shape = (WINDOWS, NLON, LEV, LAT)
    window_trend = jnp.arange(WINDOWS, dtype=jnp.float32) / max(WINDOWS - 1, 1)
    column_trend = jnp.arange(NLON, dtype=jnp.float32) / NLON
    trend = jnp.exp(0.6931472 * (window_trend[:, None, None, None] + column_trend[None, :, None, None]))
    roughness = jnp.exp(2.3025851 * jax.random.uniform(scale_key, (1, 1, LEV, LAT), jnp.float32))
    random_part = jnp.clip(jax.random.normal(random_key, full_shape, jnp.float32), -4.0, 4.0)
    return 0.15 * trend * roughness * random_part


def draw_obs_count(key, part):
    key = jax.random.fold_in(key, 29)
    count_key, first_key, second_key = jax.random.split(key, 3)
    tile_total = WINDOWS * TILES
    counts = jax.random.randint(count_key, (tile_total,), OBS_DEV // 2, OBS_DEV + 1, dtype=jnp.int32)
    full_slot = jax.random.randint(first_key, (), 0, tile_total, dtype=jnp.int32)
    half_slot = (full_slot + 1 + jax.random.randint(second_key, (), 0, tile_total - 1, dtype=jnp.int32)) % tile_total
    counts = counts.at[full_slot].set(OBS_DEV).at[half_slot].set(OBS_DEV // 2)
    return counts.reshape(WINDOWS, TILES)


def plant(result, key, least, top_value):
    index_at = [jax.random.randint(jax.random.fold_in(key, axis), (), 0, length) for axis, length in enumerate(result.shape)]
    main_axis = result.shape.index(max(result.shape))
    beside = index_at[:main_axis] + [(index_at[main_axis] + 1) % result.shape[main_axis]] + index_at[main_axis + 1:]
    return result.at[tuple(index_at)].set(least).at[tuple(beside)].set(top_value)


def levels(own_key, shape, cuts, smallest, high):
    gain, own = 1.0, jax.random.fold_in(own_key, 6)
    for position, shards_of in cuts:
        heights = jnp.exp(jax.random.uniform(jax.random.fold_in(own, position), (shards_of,), jnp.float32, smallest / len(cuts), high / len(cuts)))
        gain = gain * jnp.repeat(heights, shape[position] // shards_of).reshape([-1 if axis == position else 1 for axis in range(len(shape))])
    return gain


def normal_values(rng, dims, scale, limit, pieces=(), held_as=jnp.bfloat16):
    values = scale * jax.random.normal(rng, dims, jnp.float32)
    if pieces:
        values = values * levels(rng, dims, pieces, -0.22, 0.18)
    return jnp.clip(values, -limit, limit).astype(held_as)


def setup_inputs(seed: int = 0) -> dict:
    key_of = jax.random.split(jax.random.key(seed), 11)
    model_departure = draw_model_departure(jax.random.fold_in(key_of[10], 71), 0)
    obs_departure = normal_values(key_of[1], (WINDOWS, TILES * OBS_DEV), 1.0, 6.0, ((0, 8), (1, 64)), jnp.float32)
    obs_variance = jnp.clip(jnp.exp(math.log(2.0) - 1.3862944 * jax.random.uniform(key_of[2], (WINDOWS, TILES * OBS_DEV), jnp.float32) ** levels(key_of[2], (WINDOWS, TILES * OBS_DEV), ((0, 8), (1, 64)), -0.2, 0.2)), 0.5, 2.0)
    obs_weight = normal_values(key_of[3], (WINDOWS, LEV, TILES * OBS_DEV), LEV ** -0.5, 2.0, ((0, 8), (2, 64)), jnp.float32)
    obs_index = plant(jax.random.randint(key_of[4], (WINDOWS, TILES * OBS_DEV), 0, LON_DEV * LAT), jax.random.fold_in(key_of[4], 1), 0, (LON_DEV * LAT) - 1).astype(jnp.int32)
    obs_count = draw_obs_count(jax.random.fold_in(key_of[10], 71), 0)
    courant = jnp.clip(0.3 + 0.65 * jax.random.uniform(key_of[6], (WINDOWS, NLON, LEV, LAT), jnp.float32) ** levels(key_of[6], (WINDOWS, NLON, LEV, LAT), ((0, 8), (1, 64)), -0.2, 0.2), 0.3, 0.95)
    diffusion = jnp.clip(0.02 + 0.42999999 * jax.random.uniform(key_of[7], (WINDOWS, LEV, LAT), jnp.float32) ** levels(key_of[7], (WINDOWS, LEV, LAT), ((0, 8),), -0.2, 0.2), 0.02, 0.45)
    vertical_mix = normal_values(key_of[8], (WINDOWS, LEV, LEV), (9 * LEV) ** -0.5, 0.75, ((0, 8),), jnp.float32)
    error_variance = jnp.clip(jnp.exp(math.log(2.0) - 2.3025851 * jax.random.uniform(key_of[9], (WINDOWS, NLON, LEV * LAT), jnp.float32) ** levels(key_of[9], (WINDOWS, NLON, LEV * LAT), ((0, 8), (2, 64)), -0.2, 0.2)), 0.2, 2.0)
    return {"model_departure": model_departure, "obs_departure": obs_departure, "obs_variance": obs_variance, "obs_weight": obs_weight, "obs_index": obs_index, "obs_count": obs_count, "courant": courant, "diffusion": diffusion, "vertical_mix": vertical_mix, "error_variance": error_variance}


HALF_ROOT = 0.7071067811865476
PRECISION = lax.Precision.HIGHEST


def wavelet_forward(values, first_level, last_level):
    length, columns = values.shape
    for level_index in range(first_level, last_level + 1):
        block_size = 2 ** level_index
        shaped = values.reshape(length // block_size, 2, block_size // 2, columns)
        lower_part = shaped[:, 0, 0]
        upper_part = shaped[:, 1, 0]
        shaped = shaped.at[:, 0, 0].set((lower_part + upper_part) * HALF_ROOT)
        shaped = shaped.at[:, 1, 0].set((lower_part - upper_part) * HALF_ROOT)
        values = shaped.reshape(length, columns)
    return values


def wavelet_inverse(values, first_level, last_level):
    length, columns = values.shape
    for level_index in range(last_level, first_level - 1, -1):
        block_size = 2 ** level_index
        shaped = values.reshape(length // block_size, 2, block_size // 2, columns)
        coarse = shaped[:, 0, 0]
        detail = shaped[:, 1, 0]
        shaped = shaped.at[:, 0, 0].set((coarse + detail) * HALF_ROOT)
        shaped = shaped.at[:, 1, 0].set((coarse - detail) * HALF_ROOT)
        values = shaped.reshape(length, columns)
    return values


def advection_weights(courant):
    squared = courant * courant
    return (squared + courant) * 0.5, 1.0 - squared, (squared - courant) * 0.5


def meridional(values, diffusion):
    fluxes = diffusion[:, :-1] * (values[..., 1:] - values[..., :-1])
    border = jnp.zeros_like(values[..., :1])
    return values + jnp.concatenate([fluxes, border], axis=-1) - jnp.concatenate([border, fluxes], axis=-1)


def vertical(values, mixing):
    return jnp.einsum("lm,nmj->nlj", mixing, values, precision=PRECISION)


def vertical_adjoint(values, mixing):
    return jnp.einsum("ml,nmj->nlj", mixing, values, precision=PRECISION)


def tangent_window(packed):
    state, courant, diffusion, mixing = packed
    west_weight, centre_weight, east_weight = advection_weights(courant)
    for step_index in range(STEPS):
        advected = west_weight * jnp.roll(state, 1, axis=0) + centre_weight * state + east_weight * jnp.roll(state, -1, axis=0)
        state = vertical(meridional(advected, diffusion), mixing)
    return state


def adjoint_window(packed):
    state, courant, diffusion, mixing = packed
    west_weight, centre_weight, east_weight = advection_weights(courant)
    for step_index in range(STEPS):
        spread_out = meridional(vertical_adjoint(state, mixing), diffusion)
        state = centre_weight * spread_out + jnp.roll(west_weight * spread_out, -1, axis=0) + jnp.roll(east_weight * spread_out, 1, axis=0)
    return state


def covary_window(packed):
    values, variance = packed
    return wavelet_inverse(wavelet_forward(values, 1, HAAR) * variance, 1, HAAR)


def reference(model_departure, obs_departure, obs_variance, obs_weight, obs_index, obs_count, courant, diffusion, vertical_mix, error_variance):
    mixing = 0.7 * jnp.eye(LEV, dtype=jnp.float32)[None] + vertical_mix
    slot_ids = jnp.arange(TILES * OBS_DEV, dtype=jnp.int32)
    tile_ids = slot_ids // OBS_DEV
    live_slots = ((slot_ids % OBS_DEV)[None, :] < obs_count[:, tile_ids]).astype(jnp.float32)
    lon_index = tile_ids[None, :] * LON_DEV + obs_index // LAT
    lat_index = obs_index % LAT
    window_ids = jnp.arange(WINDOWS, dtype=jnp.int32)[:, None]

    def observe(state):
        picked = state[window_ids, lon_index, :, lat_index]
        return jnp.einsum("wol,wlo->wo", picked, obs_weight, precision=PRECISION) * live_slots

    def spread_obs(values):
        terms = jnp.swapaxes(obs_weight * values[:, None, :], 1, 2)
        return jnp.zeros_like(model_departure).at[window_ids, lon_index, :, lat_index].add(terms)

    def lagged(state):
        images = lax.map(tangent_window, (state, courant, diffusion, mixing))
        earlier = jnp.concatenate([jnp.zeros_like(images[:1]), images[:-1]], axis=0)
        return state - earlier

    def lagged_adjoint(state):
        later_state = jnp.concatenate([state[1:], jnp.zeros_like(state[:1])], axis=0)
        return state - lax.map(adjoint_window, (later_state, courant, diffusion, mixing))

    def covary(state):
        flattened = state.reshape(WINDOWS, NLON, LEV * LAT)
        return lax.map(covary_window, (flattened, error_variance)).reshape(state.shape)

    multiplier = jnp.zeros_like(model_departure)
    obs_multiplier = jnp.zeros_like(obs_departure)
    increment = jnp.zeros_like(model_departure)
    res_lam = model_departure
    res_obs = live_slots * obs_departure
    res_state = jnp.zeros_like(model_departure)
    for iter_index in range(ITERS):
        covaried = covary(res_state)
        search_lam = res_state
        search_obs = res_obs / obs_variance
        search_state = res_lam - covaried
        image_lam = covaried + lagged(search_state)
        image_obs = res_obs + observe(search_state)
        image_state = lagged_adjoint(search_lam) + spread_obs(search_obs)
        numerator = jnp.sum(res_lam * image_lam) + jnp.sum(res_obs * image_obs) + jnp.sum(res_state * image_state)
        denominator = jnp.sum(image_lam * image_lam) + jnp.sum(image_obs * image_obs) + jnp.sum(image_state * image_state) + 1e-6
        step_size = numerator / denominator
        multiplier = multiplier + step_size * search_lam
        obs_multiplier = obs_multiplier + step_size * search_obs
        increment = increment + step_size * search_state
        res_lam = res_lam - step_size * image_lam
        res_obs = res_obs - step_size * image_obs
        res_state = res_state - step_size * image_state
    return multiplier, obs_multiplier, increment
```

```python
import jax
import jax.numpy as jnp
from jax import lax
from jax.experimental import pallas as pl
from jax.experimental.pallas import tpu as pltpu
from jax.sharding import PartitionSpec as P

MESH = pl.DeviceIdType.MESH
F32 = jnp.float32
BF16 = jnp.bfloat16
LON, LEV, LAT, SLOTS = 16, 8, 384, 2048
WINDOWS, TILES, SIDE = 8, 64, 8
HALO = 4
WIDE = LON + 2 * HALO + 2
CHUNK = 512
COLUMNS = TILES * LON * LEV * LAT // (TILES * TILES * LON)


def kernel(
    md, od, ov, ow, oi, oc, cr, df, vm, ev,
    mult, omult, incr,
    ac, wts, onehot, lonb, obs, oiv, wv, dfv, vmv, latc, mixf, mixb,
    gb, gx, bufa, bufb, bufg, mo, ma, mdd, mtg, htq, bb, cb, dx,
    hb, cu, r1, s2, r2, vb, al, arr,
    sem_load, sem_hs, sem_hr, sem_1s, sem_1r, sem_2s, sem_2r, sem_cs, sem_cr, sem_gs, sem_gr, sem_ts, sem_tr, sem_as, sem_ar,
):
    k = lax.axis_index("tm")
    t = lax.axis_index("space")
    p, q = t // SIDE, t % SIDE
    east, west = (t + 1) % TILES, (t + TILES - 1) % TILES
    later, before = (k + 1) % WINDOWS, (k + WINDOWS - 1) % WINDOWS

    def send(src, dst, ssem, rsem, kk, tt):
        return pltpu.make_async_remote_copy(
            src_ref=src, dst_ref=dst, send_sem=ssem, recv_sem=rsem, device_id=(kk, tt), device_id_type=MESH
        )

    loads = [
        pltpu.make_async_copy(src, dst, sem_load.at[n])
        for n, (src, dst) in enumerate(
            [
                (md, ac.at[0, pl.ds(HALO, LON)]),
                (cr, ac.at[1, pl.ds(HALO, LON)]),
                (oi, oiv),
                (od, obs.at[0]),
                (ov, obs.at[1]),
                (ow, wv),
                (df, dfv),
                (vm, vmv),
            ]
        )
    ]
    for load in loads:
        load.start()

    barrier = pltpu.get_barrier_semaphore()

    def greet(kk, tt):
        pl.semaphore_signal(barrier, inc=1, device_id=(kk, tt), device_id_type=MESH)

    greet(k, east)
    greet(k, west)
    greet(later, east)
    greet(later, west)
    for j in range(1, SIDE):
        greet(k, p * SIDE + (q + j) % SIDE)
        greet(k, ((p + j) % SIDE) * SIDE + q)
        greet((k + j) % WINDOWS, t)
    for lev in range(LEV):

        @pl.when(lev * SIDE + p != t)
        def _():
            greet(k, lev * SIDE + p)

    for load in loads:
        load.wait()

    index = oiv[...]
    lon = (index * 10923) >> 22
    lat = index - lon * LAT
    lonb[...] = jnp.broadcast_to(lon, (LEV, SLOTS))
    for c in range(SLOTS // CHUNK):
        cols = pl.ds(c * CHUNK, CHUNK)
        rows = lax.broadcasted_iota(jnp.int32, (LAT, CHUNK), 0)
        onehot[:, cols] = jnp.where(rows == lat[:, c * CHUNK : (c + 1) * CHUNK], 1.0, 0.0).astype(BF16)
    live = lax.broadcasted_iota(jnp.int32, (1, SLOTS), 1) < oc[0, 0]
    o0 = jnp.where(live, obs[0], 0.0)
    s1 = o0 / obs[1]
    obs[0] = o0
    obs[2] = s1

    def pieces(x):
        high = x.astype(BF16)
        return high, (x - high.astype(F32)).astype(BF16)

    def spread(row, out):
        total = jnp.zeros((LON * LEV, LAT), F32)
        for c in range(SLOTS // CHUNK):
            cols = pl.ds(c * CHUNK, CHUNK)
            terms = wv[:, cols] * obs[row, :, cols]
            ids = lax.broadcasted_iota(jnp.int32, (LON, LEV, CHUNK), 0)
            placed = jnp.where(ids == lonb[:, cols][None], terms[None], 0.0).reshape(LON * LEV, CHUNK)
            for piece in pieces(placed):
                total += lax.dot_general(piece, onehot[:, cols], (((1,), (1,)), ((), ())), preferred_element_type=F32)
        out[...] = total.reshape(LON, LEV, LAT)

    def observe(field, row):
        high, low = pieces(field.reshape(LON * LEV, LAT))
        for c in range(SLOTS // CHUNK):
            cols = pl.ds(c * CHUNK, CHUNK)
            picked = jnp.dot(high, onehot[:, cols], preferred_element_type=F32)
            picked += jnp.dot(low, onehot[:, cols], preferred_element_type=F32)
            picked = picked.reshape(LON, LEV, CHUNK)
            here = lonb[:, cols]
            column = jnp.zeros((LEV, CHUNK), F32)
            for i in range(LON):
                column = jnp.where(here == i, picked[i], column)
            total = jnp.sum(column * wv[:, cols], axis=0, keepdims=True)
            slot = lax.broadcasted_iota(jnp.int32, (1, CHUNK), 1) + c * CHUNK
            obs[row, :, cols] = jnp.where(slot < oc[0, 0], total, 0.0)

    pl.semaphore_wait(barrier, 32 + jnp.where(p == q, 0, 1))

    halo = [
        send(ac.at[:, pl.ds(HALO, HALO)], ac.at[:, pl.ds(HALO + LON, HALO)], sem_hs.at[0], sem_hr.at[0], k, west),
        send(ac.at[:, pl.ds(LON, HALO)], ac.at[:, pl.ds(0, HALO)], sem_hs.at[1], sem_hr.at[1], k, east),
    ]
    for copy in halo:
        copy.start()

    first = []
    for j in range(1, SIDE):
        peer = (q + j) % SIDE
        back = (q + SIDE - j) % SIDE
        out = send(
            ev.at[:, pl.ds(pl.multiple_of(peer * 128, 128), 128)], r1.at[q], sem_1s.at[j], sem_1r.at[j], k, p * SIDE + peer
        )
        out.start()
        came = send(ev.at[:, pl.ds(0, 128)], r1.at[back], sem_1s.at[j], sem_1r.at[j], k, p * SIDE + back)
        first.append((out, came))
    own_first = pltpu.make_async_copy(ev.at[:, pl.ds(pl.multiple_of(q * 128, 128), 128)], r1.at[q], sem_1r.at[0])
    own_first.start()

    spread(2, gb)
    gsend = [
        send(gb, gx.at[pl.ds(HALO, LON)], sem_gs.at[0], sem_gr.at[0], before, t),
        send(gb.at[pl.ds(0, HALO)], gx.at[pl.ds(HALO + LON, HALO)], sem_gs.at[1], sem_gr.at[1], before, west),
        send(gb.at[pl.ds(LON - HALO, HALO)], gx.at[pl.ds(0, HALO)], sem_gs.at[2], sem_gr.at[2], before, east),
    ]
    for copy in gsend:
        copy.start()

    level_ids = lax.broadcasted_iota(jnp.int32, (LEV, LEV), 0)
    other_ids = lax.broadcasted_iota(jnp.int32, (LEV, LEV), 1)
    mixing = vmv[0] + jnp.where(level_ids == other_ids, 0.7, 0.0).astype(F32)
    for r in range(LEV):
        chosen = jnp.where(other_ids == (level_ids + r) % LEV, mixing, 0.0)
        mixf[r] = jnp.broadcast_to(jnp.sum(chosen, axis=1, keepdims=True), (LEV, LAT))
    mixb[0] = mixf[0]
    for r in range(1, LEV):
        mixb[r] = pltpu.roll(mixf[LEV - r], LEV - r, 0)
    lanes = lax.broadcasted_iota(jnp.int32, (LEV, LAT), 1)
    dn = jnp.where(lanes < LAT - 1, dfv[0], 0.0)
    dp = pltpu.roll(dn, 1, 1)
    latc[0] = dn
    latc[1] = dp
    latc[2] = 1.0 - dn - dp

    for copy in halo:
        copy.wait()

    def weigh(n, carry):
        cols = pl.ds(4 * n, 4)
        c = ac[1, cols]
        sq = c * c
        wts[0, cols] = (sq + c) * 0.5
        wts[1, cols] = 1.0 - sq
        wts[2, cols] = (sq - c) * 0.5
        return carry

    lax.fori_loop(0, 6, weigh, 0)

    def latitude(a):
        return latc[2] * a + latc[0] * pltpu.roll(a, LAT - 1, 2) + latc[1] * pltpu.roll(a, 1, 2)

    def couple(b, mix):
        total = mix[0] * b
        for r in range(1, LEV):
            total += mix[r] * pltpu.roll(b, LEV - r, 1)
        return total

    def forward(start, out):
        path = [(start, bufa, 0), (bufa, bufb, 0), (bufb, bufa, 0), (bufa, out, HALO)]
        for step, ((src, dst, off), blocks) in enumerate(zip(path, (6, 5, 5, 4))):

            def block(n, carry):
                i = step + 1 + 4 * n
                u = src[pl.ds(i - 1, 6)]
                a = wts[0, pl.ds(i, 4)] * u[0:4] + wts[1, pl.ds(i, 4)] * u[1:5] + wts[2, pl.ds(i, 4)] * u[2:6]
                dst[pl.ds(i - off, 4)] = couple(latitude(a), mixf)
                return carry

            lax.fori_loop(0, blocks, block, 0)

    def backward(start, out):
        path = [(start, bufa, 0), (bufa, bufb, 0), (bufb, bufa, 0), (bufa, out, HALO)]
        for step, ((src, dst, off), wide, narrow) in enumerate(zip(path, (6, 6, 5, 5), (6, 5, 5, 4))):

            def inner(n, carry):
                i = step + 4 * n
                bufg[pl.ds(i, 4)] = latitude(couple(src[pl.ds(i, 4)], mixb))
                return carry

            def outer(n, carry):
                i = step + 1 + 4 * n
                z = wts[1, pl.ds(i, 4)] * bufg[pl.ds(i, 4)]
                z += wts[0, pl.ds(i + 1, 4)] * bufg[pl.ds(i + 1, 4)]
                z += wts[2, pl.ds(i - 1, 4)] * bufg[pl.ds(i - 1, 4)]
                dst[pl.ds(i - off, 4)] = z
                return carry

            lax.fori_loop(0, wide, inner, 0)
            lax.fori_loop(0, narrow, outer, 0)

    forward(ac.at[0], mo.at[0])
    shift = [
        send(mo.at[0], ma, sem_ts.at[0], sem_tr.at[0], later, t),
        send(mo.at[1], mdd, sem_ts.at[1], sem_tr.at[1], later, t),
    ]
    shift[0].start()

    place = t % 4
    base = t - place
    for lt in range(LAT // 128):
        sl = pl.ds(lt * 128, 128)
        x = gb[:, :, sl]
        for n, off in ((8, 0), (4, 8), (2, 12), (1, 14)):
            pair = x.reshape(n, 2, LEV, 128)
            hb[pl.ds(off, n), :, sl] = pair[:, 0] - pair[:, 1]
            x = pair[:, 0] + pair[:, 1]
        cu[pl.ds(place, 1), :, sl] = x
    coarse = []
    for j in range(1, 4):
        peer, back = (place + j) % 4, (place + 4 - j) % 4
        out = send(cu.at[place], cu.at[place], sem_cs.at[j], sem_cr.at[j], k, base + peer)
        out.start()
        coarse.append((out, send(cu.at[place], cu.at[back], sem_cs.at[j], sem_cr.at[j], k, base + back)))

    own_first.wait()
    for out, came in first:
        out.wait_send()
        came.wait_recv()
    turned = jnp.transpose(r1[...].reshape(LAT, 128))
    s2[:, 0:LON, :] = turned.reshape(SIDE, LON, LAT)
    for g in range(2):
        rows = [s2[4 * g + j, 0:1, :] for j in range(4)]
        tops = jnp.concatenate(rows + [jnp.zeros((4, LAT), F32)], axis=0)
        for j in range(4):
            s2[4 * g + j, LON : LON + 8, :] = tops
    for s in range(SIDE):
        tile = q * SIDE + s
        out = send(s2.at[s], r2.at[p], sem_2s.at[s], sem_2r.at[p], k, tile)
        stay = pltpu.make_async_copy(s2.at[s], r2.at[p], sem_2r.at[p])

        @pl.when(tile != t)
        def _():
            out.start()

        @pl.when(tile == t)
        def _():
            stay.start()
            stay.wait()

    observe(ac[0, pl.ds(HALO, LON)], 3)
    q1 = obs[0] + obs[3]
    obs[3] = q1
    obs[4] = q1 / obs[1]
    spread(4, htq)

    for out, came in coarse:
        out.wait_send()
        came.wait_recv()
    for lev in range(LEV):
        came = send(s2.at[0], r2.at[lev], sem_2s.at[lev], sem_2r.at[lev], k, lev * SIDE + p)

        @pl.when(lev * SIDE + p != t)
        def _():
            came.wait_recv()

    vb[...] = jnp.swapaxes(r2[...], 0, 1)
    for lt in range(LAT // 128):
        sl = pl.ds(lt * 128, 128)
        u = [cu[j, :, sl] for j in range(4)]
        v = [vb[LON + j, :, sl] for j in range(4)]
        a0, d1, a2, d3 = u[0] + u[1], u[0] - u[1], u[2] + u[3], u[2] - u[3]
        top, bot = (a0 + a2) * v[0] * (1 / 64), (a0 - a2) * v[2] * (1 / 64)
        fine = jnp.where(place < 2, d1 * v[1], d3 * v[3]) * (1 / 32)
        x = jnp.where(place < 2, top + bot, top - bot) + jnp.where(place % 2 == 0, fine, -fine)
        x = x[None]
        for n, off, half in ((1, 14, 1 / 16), (2, 12, 1 / 8), (4, 8, 1 / 4), (8, 0, 1 / 2)):
            width = LON // n
            var = vb[pl.ds(0, LON), :, sl].reshape(n, width, LEV, 128)[:, width // 2]
            d = hb[pl.ds(off, n), :, sl] * var * half
            x = jnp.stack([x + d, x - d], axis=1).reshape(2 * n, LEV, 128)
        cb[:, :, sl] = x

    for copy in gsend:
        copy.wait()
    backward(gx, mtg)

    zero = jnp.zeros((LEV, LAT), F32)

    def fold(x):
        x = jnp.sum(x, axis=0, keepdims=True)
        return sum(x[:, n : n + 128] for n in range(0, x.shape[1], 128))

    def tile_of(num, den):
        row = lax.broadcasted_iota(jnp.int32, (8, 128), 0)
        return jnp.where(row == 0, num, jnp.where(row == 1, den, 0.0))

    def sum_start(which, stage, value):
        me = (q, p, k)[stage]
        arr[which, stage, me] = value
        pending = []
        for j in range(1, SIDE):
            peer, back = (me + j) % SIDE, (me + SIDE - j) % SIDE
            where = [(k, p * SIDE + peer), (k, peer * SIDE + q), (peer, t)][stage]
            whence = [(k, p * SIDE + back), (k, back * SIDE + q), (back, t)][stage]
            slot = arr.at[which, stage, me]
            sems = sem_as.at[which, stage, j], sem_ar.at[which, stage, j]
            out = send(slot, slot, *sems, *where)
            out.start()
            pending.append((out, send(slot, arr.at[which, stage, back], *sems, *whence)))
        return pending

    def sum_finish(which, stage, pending):
        for out, came in pending:
            out.wait_send()
            came.wait_recv()
        return jnp.sum(arr[which, stage], axis=0)

    def ratio(total):
        sums = jnp.sum(total, axis=1, keepdims=True)
        return sums[0:1] / (sums[1:2] + 1e-6)

    shift[0].wait()

    def differ(n, acc):
        cols = pl.ds(4 * n, 4)
        inside = pl.ds(4 * n + HALO, 4)
        a = ac[0, inside]
        b = a - jnp.where(k > 0, ma[cols], 0.0)
        bb[cols] = b
        dx[inside] = b - cb[cols]
        g = gb[cols]
        return acc[0] + jnp.sum(a * b, axis=0), acc[1] + jnp.sum(b * b + g * g, axis=0)

    num, den = lax.fori_loop(0, 4, differ, (zero, zero))
    edge = [
        send(dx.at[pl.ds(HALO, HALO)], dx.at[pl.ds(HALO + LON, HALO)], sem_hs.at[2], sem_hr.at[2], k, west),
        send(dx.at[pl.ds(LON, HALO)], dx.at[pl.ds(0, HALO)], sem_hs.at[3], sem_hr.at[3], k, east),
    ]
    for copy in edge:
        copy.start()
    q1 = obs[3]
    pending = sum_start(0, 0, tile_of(fold(num) + fold(obs[0] * q1), fold(den) + fold(q1 * q1)))

    observe(dx[pl.ds(HALO, LON)], 5)

    for copy in edge:
        copy.wait()
    forward(dx, mo.at[1])
    shift[1].start()

    total = sum_finish(0, 0, pending)
    pending = sum_start(0, 1, total)
    total = sum_finish(0, 1, pending)
    pending = sum_start(0, 2, total)
    total = sum_finish(0, 2, pending)
    al[0] = jnp.broadcast_to(ratio(total), (LEV, LAT))
    alpha = al[0]
    alpha1 = al[0, 0:1, 0:1]

    q1 = obs[3]
    q_obs = q1 - alpha1 * (q1 + obs[5])
    r_obs = obs[0] - alpha1 * q1

    def state_part(n, acc):
        cols = pl.ds(4 * n, 4)
        g = gb[cols]
        qs = g - alpha * (g - jnp.where(k < WINDOWS - 1, mtg[cols], 0.0) + htq[cols])
        return acc[0] - jnp.sum(alpha * g * qs, axis=0), acc[1] + jnp.sum(qs * qs, axis=0)

    acc = lax.fori_loop(0, 4, state_part, (zero, zero))
    shift[1].wait()

    def lam_part(n, acc):
        cols = pl.ds(4 * n, 4)
        inside = pl.ds(4 * n + HALO, 4)
        b = bb[cols]
        ql = b - alpha * (cb[cols] + dx[inside] - jnp.where(k > 0, mdd[cols], 0.0))
        rl = ac[0, inside] - alpha * b
        return acc[0] + jnp.sum(rl * ql, axis=0), acc[1] + jnp.sum(ql * ql, axis=0)

    num, den = lax.fori_loop(0, 4, lam_part, acc)
    total = tile_of(fold(num) + fold(r_obs * q_obs), fold(den) + fold(q_obs * q_obs))
    for stage in range(3):
        pending = sum_start(1, stage, total)
        total = sum_finish(1, stage, pending)
    beta = ratio(total)
    al[1] = jnp.broadcast_to(beta, (LEV, LAT))
    beta = al[1]

    def write(n, carry):
        cols = pl.ds(4 * n, 4)
        inside = pl.ds(4 * n + HALO, 4)
        a = ac[0, inside]
        mult[0, cols] = -(alpha * beta) * gb[cols]
        incr[0, cols] = alpha * a + beta * (a - alpha * dx[inside])
        return carry

    lax.fori_loop(0, 4, write, 0)
    beta1 = al[1, 0:1, 0:1]
    s1 = obs[2]
    omult[...] = alpha1 * s1 + beta1 * (s1 - alpha1 * obs[4])

    for s in range(SIDE):
        out = send(s2.at[s], r2.at[p], sem_2s.at[s], sem_2r.at[p], k, q * SIDE + s)

        @pl.when(q * SIDE + s != t)
        def _():
            out.wait_send()


def field(*lead):
    return pltpu.VMEM((*lead, LEV, LAT), F32)


SCRATCH = [
    field(2, WIDE),
    field(3, WIDE),
    pltpu.VMEM((LAT, SLOTS), BF16),
    pltpu.VMEM((LEV, SLOTS), jnp.int32),
    pltpu.VMEM((6, 1, SLOTS), F32),
    pltpu.VMEM((1, SLOTS), jnp.int32),
    pltpu.VMEM((LEV, SLOTS), F32),
    field(1),
    pltpu.VMEM((1, LEV, LEV), F32),
    field(3),
    field(LEV),
    field(LEV),
    field(LON),
    field(WIDE),
    field(WIDE),
    field(WIDE),
    field(WIDE),
    field(2, LON),
    field(LON),
    field(LON),
    field(LON),
    field(LON),
    field(LON),
    field(LON),
    field(WIDE),
    field(LON),
    field(4),
    pltpu.VMEM((SIDE, LAT // SIDE, 128), F32),
    pltpu.VMEM((SIDE, LON + 8, LAT), F32),
    pltpu.VMEM((LEV, LON + 8, LAT), F32),
    field(LON + 8),
    field(2),
    pltpu.VMEM((2, 3, SIDE, 8, 128), F32),
] + [
    pltpu.SemaphoreType.DMA(shape)
    for shape in (
        (8,), (4,), (4,), (8,), (8,), (8,), (8,), (4,), (4,), (3,), (3,), (2,), (2,), (2, 3, 8), (2, 3, 8),
    )
]


def body(md, od, ov, ow, oi, oc, cr, df, vm, ev):
    hbm = pl.BlockSpec(memory_space=pl.ANY)
    vmem = pl.BlockSpec(memory_space=pltpu.VMEM)
    return pl.pallas_call(
        kernel,
        out_shape=(
            jax.ShapeDtypeStruct((1, LON, LEV, LAT), F32),
            jax.ShapeDtypeStruct((1, SLOTS), F32),
            jax.ShapeDtypeStruct((1, LON, LEV, LAT), F32),
        ),
        in_specs=[hbm] * 5 + [pl.BlockSpec(memory_space=pltpu.SMEM)] + [hbm] * 4,
        out_specs=(vmem, vmem, vmem),
        scratch_shapes=SCRATCH,
        compiler_params=pltpu.CompilerParams(
            collective_id=0, has_side_effects=True, vmem_limit_bytes=48 * 1024 * 1024
        ),
        name="saddle",
    )(md[0], od, ov, ow[0], oi, oc, cr[0], df, vm, jnp.swapaxes(ev[0], 0, 1))


def solution(mesh):
    in_specs = (
        P("tm", "space", None, None),
        P("tm", "space"),
        P("tm", "space"),
        P("tm", None, "space"),
        P("tm", "space"),
        P("tm", "space"),
        P("tm", "space", None, None),
        P("tm", None, None),
        P("tm", None, None),
        P("tm", None, "space"),
    )
    out_specs = (P("tm", "space", None, None), P("tm", "space"), P("tm", "space", None, None))
    return jax.shard_map(body, mesh=mesh, in_specs=in_specs, out_specs=out_specs, check_vma=False)
```

```python
import jax
import jax.numpy as jnp
from jax import lax
from jax.experimental import pallas as pl
from jax.experimental.pallas import tpu as pltpu
from jax.sharding import PartitionSpec as P

MESH = pl.DeviceIdType.MESH
F32 = jnp.float32
BF16 = jnp.bfloat16
LON, LEV, LAT, SLOTS = 16, 8, 384, 2048
WINDOWS, TILES, SIDE = 8, 64, 8
HALO = 4
WIDE = LON + 2 * HALO + 2
CHUNK = 512
FAR_FIRST = (4, 3, 5, 2, 6, 1, 7)


def kernel(
    md, od, ov, ow, oi, oc, cr, df, vm, ev,
    mult, omult, incr,
    ac, wts, onehot, lonb, obs, oiv, ocv, wv, dfv, vmv, latc, mixf, mixb,
    gb, gx, bufa, bufb, bufg, mo, ma, an, mtg, htq, bb, cb, dx,
    hb, cu, evv, evp, r1, tops, s2, r2, vt, vb, al, arr,
    sem_load, sem_hs, sem_hr, sem_1s, sem_1r, sem_2s, sem_2r, sem_cs, sem_cr, sem_gs, sem_gr, sem_ts, sem_tr, sem_as, sem_ar,
):
    k = lax.axis_index("tm")
    t = lax.axis_index("space")
    x, zl = k // 2, k % 2
    zh, y, c = t // 16, t // 2 % 8, t % 2
    east, west = (t + 1) % TILES, (t + TILES - 1) % TILES
    later, before = (k + 1) % WINDOWS, (k + WINDOWS - 1) % WINDOWS
    place = t % 4
    base = t - place

    def send(src, dst, ssem, rsem, kk, tt):
        return pltpu.make_async_remote_copy(
            src_ref=src, dst_ref=dst, send_sem=ssem, recv_sem=rsem, device_id=(kk, tt), device_id_type=MESH
        )

    def tile_at(zz, yy, cc):
        return zz * 16 + yy * 2 + cc

    def on_y(place):
        return k, tile_at(zh, place, c)

    def on_z(place):
        return x * 2 + place % 2, tile_at(place // 2, y, c)

    def on_xc(place):
        return place // 2 * 2 + zl, tile_at(zh, y, place % 2)

    def on_zc(place):
        return k, tile_at(place // 2, y, place % 2)

    loads = [
        pltpu.make_async_copy(src, dst, sem_load.at[n])
        for n, (src, dst) in enumerate(
            [
                (ev, evv),
                (oi, oiv),
                (od, obs.at[0]),
                (ov, obs.at[1]),
                (oc, ocv),
                (ow, wv),
                (md, ac.at[0, pl.ds(HALO, LON)]),
                (cr, ac.at[1, pl.ds(HALO, LON)]),
                (df, dfv),
                (vm, vmv),
            ]
        )
    ]
    for load in loads:
        load.start()

    barrier = pltpu.get_barrier_semaphore()

    def greet(kk, tt):
        pl.semaphore_signal(barrier, inc=1, device_id=(kk, tt), device_id_type=MESH)

    for j in FAR_FIRST:
        greet(*on_y((y + j) % SIDE))
        greet(*on_zc((zh * 2 + c + j) % SIDE))
    for j in range(4):
        greet(x * 2 + 1 - zl, tile_at((zh + j) % 4, y, c))
    for j in range(1, 4):
        greet((x + j) % 4 * 2 + zl, t)
        greet((x + j) % 4 * 2 + zl, t + 1 - 2 * c)
    greet(later, east)
    greet(later, west)
    greet(later, t)
    greet(before, t)
    greet(k, base + 3 - place)
    greet(k, east)
    greet(k, west)

    lane = lax.broadcasted_iota(jnp.int32, (LAT // SIDE, 128), 1)
    loads[0].wait()
    for zz in range(4):
        for cc in range(2):
            block = None
            for yy in range(SIDE):
                source = evv[:, pl.ds((zz * 2 + yy // 4) * 128, 128)]
                offset = (yy * 16 - (yy % 4 * 32 + cc * 16)) % 128
                moved = pltpu.roll(source, offset, 1) if offset else source
                block = moved if block is None else jnp.where(lane >= yy * 16, moved, block)
            evp[zz * 2 + cc] = block
    for load in loads[1:]:
        load.wait()

    index = oiv[...]
    lon = (index * 10923) >> 22
    lat = index - lon * LAT
    lonb[...] = jnp.broadcast_to(lon, (LEV, SLOTS))
    for n in range(SLOTS // CHUNK):
        cols = pl.ds(n * CHUNK, CHUNK)
        rows = lax.broadcasted_iota(jnp.int32, (LAT, CHUNK), 0)
        onehot[:, cols] = jnp.where(rows == lat[:, n * CHUNK : (n + 1) * CHUNK], 1.0, 0.0).astype(BF16)
    live = lax.broadcasted_iota(jnp.int32, (1, SLOTS), 1) < ocv[...]
    o0 = jnp.where(live, obs[0], 0.0)
    s1 = o0 / obs[1]
    obs[0] = o0
    obs[2] = s1

    def pieces(x):
        high = x.astype(BF16)
        return high, (x - high.astype(F32)).astype(BF16)

    def spread(row, out):
        total = jnp.zeros((LON * LEV, LAT), F32)
        for n in range(SLOTS // CHUNK):
            cols = pl.ds(n * CHUNK, CHUNK)
            terms = wv[:, cols] * obs[row, :, cols]
            ids = lax.broadcasted_iota(jnp.int32, (LON, LEV, CHUNK), 0)
            placed = jnp.where(ids == lonb[:, cols][None], terms[None], 0.0).reshape(LON * LEV, CHUNK)
            for piece in pieces(placed):
                total += lax.dot_general(piece, onehot[:, cols], (((1,), (1,)), ((), ())), preferred_element_type=F32)
        out[...] = total.reshape(LON, LEV, LAT)

    def observe(field, row):
        high, low = pieces(field.reshape(LON * LEV, LAT))
        for n in range(SLOTS // CHUNK):
            cols = pl.ds(n * CHUNK, CHUNK)
            picked = jnp.dot(high, onehot[:, cols], preferred_element_type=F32)
            picked += jnp.dot(low, onehot[:, cols], preferred_element_type=F32)
            picked = picked.reshape(LON, LEV, CHUNK)
            here = lonb[:, cols]
            column = jnp.zeros((LEV, CHUNK), F32)
            for i in range(LON):
                column = jnp.where(here == i, picked[i], column)
            total = jnp.sum(column * wv[:, cols], axis=0, keepdims=True)
            slot = lax.broadcasted_iota(jnp.int32, (1, CHUNK), 1) + n * CHUNK
            obs[row, :, cols] = jnp.where(slot < ocv[...], total, 0.0)

    spread(2, gb)
    for lt in range(LAT // 128):
        sl = pl.ds(lt * 128, 128)
        u = gb[:, :, sl]
        for n, off in ((8, 0), (4, 8), (2, 12), (1, 14)):
            pair = u.reshape(n, 2, LEV, 128)
            hb[pl.ds(off, n), :, sl] = pair[:, 0] - pair[:, 1]
            u = pair[:, 0] + pair[:, 1]
        cu[pl.ds(place, 1), :, sl] = u

    level_ids = lax.broadcasted_iota(jnp.int32, (LEV, LEV), 0)
    other_ids = lax.broadcasted_iota(jnp.int32, (LEV, LEV), 1)
    mixing = vmv[0] + jnp.where(level_ids == other_ids, 0.7, 0.0).astype(F32)
    for r in range(LEV):
        chosen = jnp.where(other_ids == (level_ids + r) % LEV, mixing, 0.0)
        mixf[r] = jnp.broadcast_to(jnp.sum(chosen, axis=1, keepdims=True), (LEV, LAT))
    mixb[0] = mixf[0]
    for r in range(1, LEV):
        mixb[r] = pltpu.roll(mixf[LEV - r], LEV - r, 0)
    lanes = lax.broadcasted_iota(jnp.int32, (LEV, LAT), 1)
    dn = jnp.where(lanes < LAT - 1, dfv[0], 0.0)
    dp = pltpu.roll(dn, 1, 1)
    latc[0] = dn
    latc[1] = dp
    latc[2] = 1.0 - dn - dp

    def weigh(start, count):
        cols = pl.ds(start, count)
        c = ac[1, cols]
        sq = c * c
        wts[0, cols] = (sq + c) * 0.5
        wts[1, cols] = 1.0 - sq
        wts[2, cols] = (sq - c) * 0.5

    for n in range(4):
        weigh(HALO + 4 * n, 4)

    pl.semaphore_wait(barrier, 31)

    halo = [
        send(ac.at[:, pl.ds(HALO, HALO)], ac.at[:, pl.ds(HALO + LON, HALO)], sem_hs.at[0], sem_hr.at[0], k, west),
        send(ac.at[:, pl.ds(LON, HALO)], ac.at[:, pl.ds(0, HALO)], sem_hs.at[1], sem_hr.at[1], k, east),
    ]
    for copy in halo:
        copy.start()

    me = zh * 2 + c
    first = []
    for j in FAR_FIRST:
        peer, back = (me + j) % SIDE, (me + SIDE - j) % SIDE
        out = send(evp.at[peer], r1.at[me], sem_1s.at[j], sem_1r.at[j], *on_zc(peer))
        out.start()
        first.append((out, send(evp.at[peer], r1.at[back], sem_1s.at[j], sem_1r.at[j], *on_zc(back))))
    r1[pl.ds(me, 1)] = evp[pl.ds(me, 1)]

    coarse = []
    for j in range(1, 4):
        peer, back = (place + j) % 4, (place + 4 - j) % 4
        out = send(cu.at[place], cu.at[place], sem_cs.at[j], sem_cr.at[j], k, base + peer)
        out.start()
        coarse.append((out, send(cu.at[place], cu.at[back], sem_cs.at[j], sem_cr.at[j], k, base + back)))
    gsend = [
        send(gb, gx.at[pl.ds(HALO, LON)], sem_gs.at[0], sem_gr.at[0], before, t),
        send(gb.at[pl.ds(0, HALO)], gx.at[pl.ds(HALO + LON, HALO)], sem_gs.at[1], sem_gr.at[1], before, west),
        send(gb.at[pl.ds(LON - HALO, HALO)], gx.at[pl.ds(0, HALO)], sem_gs.at[2], sem_gr.at[2], before, east),
    ]
    asend = send(ac.at[0, pl.ds(HALO, LON)], an, sem_ts.at[1], sem_tr.at[1], before, t)
    for copy in gsend:
        copy.start()

    observe(ac[0, pl.ds(HALO, LON)], 3)
    q1 = obs[0] + obs[3]
    obs[3] = q1
    obs[4] = q1 / obs[1]

    def latitude(a):
        return latc[2] * a + latc[0] * pltpu.roll(a, LAT - 1, 2) + latc[1] * pltpu.roll(a, 1, 2)

    def couple(b, mix):
        total = mix[0] * b
        for r in range(1, LEV):
            total += mix[r] * pltpu.roll(b, LEV - r, 1)
        return total

    def forward(start, out):
        path = [(start, bufa, 0), (bufa, bufb, 0), (bufb, bufa, 0), (bufa, out, HALO)]
        for step, ((src, dst, off), blocks) in enumerate(zip(path, (6, 5, 5, 4))):

            def block(n, carry):
                i = step + 1 + 4 * n
                u = src[pl.ds(i - 1, 6)]
                a = wts[0, pl.ds(i, 4)] * u[0:4] + wts[1, pl.ds(i, 4)] * u[1:5] + wts[2, pl.ds(i, 4)] * u[2:6]
                dst[pl.ds(i - off, 4)] = couple(latitude(a), mixf)
                return carry

            lax.fori_loop(0, blocks, block, 0, unroll=True)

    def backward(start, out):
        path = [(start, bufa, 0), (bufa, bufb, 0), (bufb, bufa, 0), (bufa, out, HALO)]
        for step, ((src, dst, off), wide, narrow) in enumerate(zip(path, (6, 6, 5, 5), (6, 5, 5, 4))):

            def inner(n, carry):
                i = step + 4 * n
                bufg[pl.ds(i, 4)] = latitude(couple(src[pl.ds(i, 4)], mixb))
                return carry

            def outer(n, carry):
                i = step + 1 + 4 * n
                z = wts[1, pl.ds(i, 4)] * bufg[pl.ds(i, 4)]
                z += wts[0, pl.ds(i + 1, 4)] * bufg[pl.ds(i + 1, 4)]
                z += wts[2, pl.ds(i - 1, 4)] * bufg[pl.ds(i - 1, 4)]
                dst[pl.ds(i - off, 4)] = z
                return carry

            lax.fori_loop(0, wide, inner, 0, unroll=True)
            lax.fori_loop(0, narrow, outer, 0, unroll=True)

    for copy in halo:
        copy.wait()
    weigh(0, HALO)
    weigh(HALO + LON, HALO)
    forward(ac.at[0], mo.at[0])
    shift = send(mo.at[0], ma, sem_ts.at[0], sem_tr.at[0], later, t)
    shift.start()
    asend.start()

    for out, came in first:
        came.wait_recv()
    turned = jnp.transpose(r1[...].reshape(LAT, 128))
    s2[:, 0:LON, :] = turned.reshape(SIDE, LON, LAT)
    tops[0] = jnp.concatenate([turned[n * LON : n * LON + 1] for n in range(SIDE)], axis=0)
    swap = send(tops.at[0], tops.at[1], sem_cs.at[0], sem_cr.at[0], k, t + 1 - 2 * c)
    swap.start()
    swap.wait()
    even = jnp.where(c == 0, tops[0], tops[1])
    odd = jnp.where(c == 0, tops[1], tops[0])
    for n in range(0, SIDE, 2):
        rows = [even[n : n + 1], odd[n : n + 1], even[n + 1 : n + 2], odd[n + 1 : n + 2], jnp.zeros((4, LAT), F32)]
        rows = jnp.concatenate(rows, axis=0)
        s2[n, LON : LON + 8, :] = rows
        s2[n + 1, LON : LON + 8, :] = rows
    second = []
    for j in FAR_FIRST:
        peer, back = (y + j) % SIDE, (y + SIDE - j) % SIDE
        out = send(s2.at[peer], r2.at[y], sem_2s.at[j], sem_2r.at[j], *on_y(peer))
        out.start()
        second.append((out, send(s2.at[peer], r2.at[back], sem_2s.at[j], sem_2r.at[j], *on_y(back))))
    r2[pl.ds(y, 1)] = s2[pl.ds(y, 1)]

    spread(4, htq)
    for copy in gsend:
        copy.wait()
    backward(gx, mtg)

    for out, came in coarse:
        came.wait_recv()
    for out, came in second:
        came.wait_recv()
    lane = lax.broadcasted_iota(jnp.int32, (LON + 8, LAT), 1)
    for zz in range(4):
        for half in range(2):
            level = None
            for m in range(4):
                offset = (96 * (m - zz)) % LAT
                source = r2[half * 4 + m]
                moved = pltpu.roll(source, offset, 1) if offset else source
                level = moved if level is None else jnp.where(lane >= 96 * m, moved, level)
            vt[zz * 2 + half] = level
    vb[...] = jnp.swapaxes(vt[...], 0, 1)
    for lt in range(LAT // 128):
        sl = pl.ds(lt * 128, 128)
        u = [cu[j, :, sl] for j in range(4)]
        v = [vb[LON + j, :, sl] for j in range(4)]
        a0, d1, a2, d3 = u[0] + u[1], u[0] - u[1], u[2] + u[3], u[2] - u[3]
        top, bot = (a0 + a2) * v[0] * (1 / 64), (a0 - a2) * v[2] * (1 / 64)
        fine = jnp.where(place < 2, d1 * v[1], d3 * v[3]) * (1 / 32)
        u = jnp.where(place < 2, top + bot, top - bot) + jnp.where(place % 2 == 0, fine, -fine)
        u = u[None]
        for n, off, half in ((1, 14, 1 / 16), (2, 12, 1 / 8), (4, 8, 1 / 4), (8, 0, 1 / 2)):
            width = LON // n
            var = vb[pl.ds(0, LON), :, sl].reshape(n, width, LEV, 128)[:, width // 2]
            d = hb[pl.ds(off, n), :, sl] * var * half
            u = jnp.stack([u + d, u - d], axis=1).reshape(2 * n, LEV, 128)
        cb[:, :, sl] = u

    shift.wait()

    def differ(n, carry):
        cols = pl.ds(4 * n, 4)
        inside = pl.ds(4 * n + HALO, 4)
        dx[inside] = ac[0, inside] - jnp.where(k > 0, ma[cols], 0.0) - cb[cols]
        return carry

    lax.fori_loop(0, 4, differ, 0, unroll=True)
    edge = [
        send(dx.at[pl.ds(HALO, HALO)], dx.at[pl.ds(HALO + LON, HALO)], sem_hs.at[2], sem_hr.at[2], k, west),
        send(dx.at[pl.ds(LON, HALO)], dx.at[pl.ds(0, HALO)], sem_hs.at[3], sem_hr.at[3], k, east),
    ]
    for copy in edge:
        copy.start()
    observe(dx[pl.ds(HALO, LON)], 5)

    def fold(x):
        x = jnp.sum(x, axis=0, keepdims=True)
        return sum(x[:, n : n + 128] for n in range(0, x.shape[1], 128))

    zero = jnp.zeros((LEV, LAT), F32)

    def state_part(n, acc):
        cols = pl.ds(4 * n, 4)
        g = gb[cols]
        f = g - jnp.where(k < WINDOWS - 1, mtg[cols], 0.0) + htq[cols]
        return acc[0] + jnp.sum(g * g, axis=0), acc[1] + jnp.sum(g * f, axis=0), acc[2] + jnp.sum(f * f, axis=0)

    gg, gf, ff = lax.fori_loop(0, 4, state_part, (zero, zero, zero), unroll=True)
    o0, q1 = obs[0], obs[3]
    h = q1 + obs[5]
    sums = [fold(o0 * q1), fold(gg) + fold(q1 * q1), fold(o0 * h), fold(gf) + fold(q1 * h), fold(ff) + fold(h * h)]
    asend.wait()

    for copy in edge:
        copy.wait()
    forward(dx, mo.at[1])

    def lam_part(n, acc):
        cols = pl.ds(4 * n, 4)
        a = an[cols]
        b = a - jnp.where(k < WINDOWS - 1, mo[0, cols], 0.0)
        e = b - jnp.where(k < WINDOWS - 1, mo[1, cols], 0.0)
        products = (a * b, b * b, a * e, b * e, e * e)
        return tuple(total + jnp.sum(product, axis=0) for total, product in zip(acc, products))

    acc = lax.fori_loop(0, 4, lam_part, (zero,) * 5, unroll=True)
    row = lax.broadcasted_iota(jnp.int32, (8, 128), 0)
    total = jnp.zeros((8, 128), F32)
    for n in range(5):
        total = jnp.where(row == n, sums[n] + fold(acc[n]), total)

    sent = []
    for stage, (me, ring) in enumerate(((y, on_y), (zh * 2 + zl, on_z), (x * 2 + c, on_xc))):
        arr[stage, me] = total
        pending = []
        for j in FAR_FIRST:
            peer, back = (me + j) % SIDE, (me + SIDE - j) % SIDE
            slot = arr.at[stage, me]
            sems = sem_as.at[stage, j], sem_ar.at[stage, j]
            out = send(slot, slot, *sems, *ring(peer))
            out.start()
            sent.append(out)
            pending.append(send(slot, arr.at[stage, back], *sems, *ring(back)))
        for came in pending:
            came.wait_recv()
        total = jnp.sum(arr[stage], axis=0)
    total = jnp.sum(total, axis=1, keepdims=True)
    rq, qq, re, qe, ee = (total[n : n + 1] for n in range(5))
    alpha = rq / (qq + 1e-6)
    beta = alpha * (1e-6 - re + alpha * qe) / (qq - 2.0 * alpha * qe + alpha * alpha * ee + 1e-6)
    al[0] = jnp.broadcast_to(alpha, (LEV, LAT))
    al[1] = jnp.broadcast_to(beta, (LEV, LAT))
    alpha, beta = al[0], al[1]

    def write(n, carry):
        cols = pl.ds(4 * n, 4)
        inside = pl.ds(4 * n + HALO, 4)
        a = ac[0, inside]
        mult[0, cols] = -(alpha * beta) * gb[cols]
        incr[0, cols] = alpha * a + beta * (a - alpha * dx[inside])
        return carry

    lax.fori_loop(0, 4, write, 0, unroll=True)
    alpha, beta = al[0, 0:1, 0:1], al[1, 0:1, 0:1]
    s1 = obs[2]
    omult[...] = alpha * s1 + beta * (s1 - alpha * obs[4])

    for out, came in first + second + coarse:
        out.wait_send()
    for out in sent:
        out.wait_send()


def field(*lead):
    return pltpu.VMEM((*lead, LEV, LAT), F32)


SCRATCH = [
    field(2, WIDE),
    field(3, WIDE),
    pltpu.VMEM((LAT, SLOTS), BF16),
    pltpu.VMEM((LEV, SLOTS), jnp.int32),
    pltpu.VMEM((6, 1, SLOTS), F32),
    pltpu.VMEM((1, SLOTS), jnp.int32),
    pltpu.VMEM((1, 1), jnp.int32),
    pltpu.VMEM((LEV, SLOTS), F32),
    field(1),
    pltpu.VMEM((1, LEV, LEV), F32),
    field(3),
    field(LEV),
    field(LEV),
    field(LON),
    field(WIDE),
    field(WIDE),
    field(WIDE),
    field(WIDE),
    field(2, LON),
    field(LON),
    field(LON),
    field(LON),
    field(LON),
    field(LON),
    field(LON),
    field(WIDE),
    field(LON),
    field(4),
    pltpu.VMEM((LAT // SIDE, TILES * LON), F32),
    pltpu.VMEM((SIDE, LAT // SIDE, 128), F32),
    pltpu.VMEM((SIDE, LAT // SIDE, 128), F32),
    field(2),
    pltpu.VMEM((SIDE, LON + 8, LAT), F32),
    pltpu.VMEM((SIDE, LON + 8, LAT), F32),
    pltpu.VMEM((LEV, LON + 8, LAT), F32),
    field(LON + 8),
    field(2),
    pltpu.VMEM((3, SIDE, 8, 128), F32),
] + [
    pltpu.SemaphoreType.DMA(shape)
    for shape in (
        (10,), (4,), (4,), (8,), (8,), (8,), (8,), (4,), (4,), (3,), (3,), (2,), (2,), (3, 8), (3, 8),
    )
]


def body(md, od, ov, ow, oi, oc, cr, df, vm, ev):
    hbm = pl.BlockSpec(memory_space=pltpu.HBM)
    vmem = pl.BlockSpec(memory_space=pltpu.VMEM)
    return pl.pallas_call(
        kernel,
        out_shape=(
            jax.ShapeDtypeStruct((1, LON, LEV, LAT), F32),
            jax.ShapeDtypeStruct((1, SLOTS), F32),
            jax.ShapeDtypeStruct((1, LON, LEV, LAT), F32),
        ),
        in_specs=[hbm] * 10,
        out_specs=(vmem, vmem, vmem),
        scratch_shapes=SCRATCH,
        compiler_params=pltpu.CompilerParams(
            collective_id=0, has_side_effects=True, vmem_limit_bytes=60 * 1024 * 1024
        ),
        name="saddle",
    )(md[0], od, ov, ow[0], oi, oc, cr[0], df, vm, jnp.swapaxes(ev[0], 0, 1))


def solution(mesh):
    in_specs = (
        P("tm", "space", None, None),
        P("tm", "space"),
        P("tm", "space"),
        P("tm", None, "space"),
        P("tm", "space"),
        P("tm", "space"),
        P("tm", "space", None, None),
        P("tm", None, None),
        P("tm", None, None),
        P("tm", None, "space"),
    )
    out_specs = (P("tm", "space", None, None), P("tm", "space"), P("tm", "space", None, None))
    return jax.shard_map(body, mesh=mesh, in_specs=in_specs, out_specs=out_specs, check_vma=False)
```

```python
import jax
import jax.numpy as jnp
from jax import lax
from jax.experimental import pallas as pl
from jax.experimental.pallas import tpu as pltpu
from jax.sharding import PartitionSpec as P

MESH = pl.DeviceIdType.MESH
F32 = jnp.float32
BF16 = jnp.bfloat16
LON, LEV, LAT, SLOTS = 16, 8, 384, 2048
WINDOWS, TILES, SIDE = 8, 64, 8
HALO = 4
WIDE = LON + 2 * HALO + 2
CHUNK = 512
FAR_FIRST = (4, 3, 5, 2, 6, 1, 7)
FAR_YC = (8, 7, 9, 6, 10, 5, 11, 4, 12, 3, 13, 2, 14, 1, 15)
FAR_ZX = tuple(sorted(range(1, 32), key=lambda j: (-min(j // 4, 8 - j // 4), j)))


def kernel(
    md, od, ov, ow, oi, oc, cr, df, vm, ev,
    gb, dd, ao, so, al,
    ac, wts, onehot, onehot_n, lonb, lonb_n, obs, oiv, oiv_n, wv, terms, terms_n, dfv, vmv, latc, mixf, mixb,
    gx, bufa, bufb, bufg, mo, ma, an, mtg, htq, dx,
    hb, cu, evv, evp, r1, s2, r2, vt, vb, wq, wn, up, arr1, arr2,
    sem_load, sem_hs, sem_hr, sem_1s, sem_1r, sem_2s, sem_2r, sem_ws, sem_wr, sem_cs, sem_cr, sem_gs, sem_gr, sem_ts, sem_tr, sem_a,
):
    k = lax.axis_index("tm")
    t = lax.axis_index("space")
    x, zl = k // 2, k % 2
    zh, y, c = t // 16, t // 2 % 8, t % 2
    east, west = (t + 1) % TILES, (t + TILES - 1) % TILES
    later, before = (k + 1) % WINDOWS, (k + WINDOWS - 1) % WINDOWS
    place = t % 4
    base = t - place

    def send(src, dst, ssem, rsem, kk, tt):
        return pltpu.make_async_remote_copy(
            src_ref=src, dst_ref=dst, send_sem=ssem, recv_sem=rsem, device_id=(kk, tt), device_id_type=MESH
        )

    def tile_at(zz, yy, cc):
        return zz * 16 + yy * 2 + cc

    def on_y(place):
        return k, tile_at(zh, place, c)

    def on_zc(place):
        return k, tile_at(place // 2, y, place % 2)

    def on_yc(place):
        return k, tile_at(zh, place // 2, place % 2)

    def on_zx(place):
        return place % 4 * 2 + place // 4 % 2, tile_at(place // 8, y, c)

    loads = [
        pltpu.make_async_copy(src, dst, sem_load.at[n])
        for n, (src, dst) in enumerate(
            [
                (ev, evv),
                (md, ac.at[0, pl.ds(HALO, LON)]),
                (cr, ac.at[1, pl.ds(HALO, LON)]),
                (oi, oiv),
                (od, obs.at[0]),
                (ov, obs.at[1]),
                (ow, wv),
                (df, dfv),
                (vm, vmv),
            ]
        )
    ]
    for load in loads:
        load.start()

    barrier = pltpu.get_barrier_semaphore()

    def greet(kk, tt):
        pl.semaphore_signal(barrier, inc=1, device_id=(kk, tt), device_id_type=MESH)

    me_yc, me_zx = y * 2 + c, (zh * 2 + zl) * 4 + x
    for j in FAR_ZX:
        greet(*on_zx((me_zx + j) % 32))
    for j in FAR_YC:
        greet(*on_yc((me_yc + j) % 16))
    for j in range(1, 4):
        greet(k, tile_at((zh + j) % 4, y, 1 - c))
    greet(k, east)
    greet(k, west)
    beside = jnp.where(place == 0, base + TILES - 4, base + 4) % TILES

    @pl.when((place == 0) | (place == 3))
    def _():
        for j in range(4):
            greet(k, beside + j)


    lane_v = lax.broadcasted_iota(jnp.int32, (LAT // SIDE, 128), 1)
    loads[0].wait()
    for zz in range(4):
        for cc in range(2):
            block = None
            for yy in range(SIDE):
                source = evv[:, pl.ds((zz * 2 + yy // 4) * 128, 128)]
                offset = (yy * 16 - (yy % 4 * 32 + cc * 16)) % 128
                moved = pltpu.roll(source, offset, 1) if offset else source
                block = moved if block is None else jnp.where(lane_v >= yy * 16, moved, block)
            evp[zz * 2 + cc] = block
    halo = [
        send(ac.at[:, pl.ds(HALO, HALO)], ac.at[:, pl.ds(HALO + LON, HALO)], sem_hs.at[0], sem_hr.at[0], k, west),
        send(ac.at[:, pl.ds(LON, HALO)], ac.at[:, pl.ds(0, HALO)], sem_hs.at[1], sem_hr.at[1], k, east),
    ]
    loads[1].wait()
    loads[2].wait()
    pl.semaphore_wait(barrier, 53)
    for copy in halo:
        copy.start()

    me = zh * 2 + c
    first = []
    for j in FAR_FIRST:
        peer, back = (me + j) % SIDE, (me + SIDE - j) % SIDE
        out = send(evp.at[peer], r1.at[me], sem_1s.at[j], sem_1r.at[j], *on_zc(peer))
        out.start()
        first.append((out, send(evp.at[peer], r1.at[back], sem_1s.at[j], sem_1r.at[j], *on_zc(back))))
    r1[pl.ds(me, 1)] = evp[pl.ds(me, 1)]

    for load in loads[3:]:
        load.wait()

    def place_slots(index, lon_out, hot_out):
        lon = (index * 10923) >> 22
        lat = index - lon * LAT
        lon_out[...] = jnp.broadcast_to(lon, (LEV, SLOTS))
        for n in range(SLOTS // CHUNK):
            rows = lax.broadcasted_iota(jnp.int32, (LAT, CHUNK), 0)
            hot = jnp.where(rows == lat[:, n * CHUNK : (n + 1) * CHUNK], 1.0, 0.0)
            hot_out[:, pl.ds(n * CHUNK, CHUNK)] = hot.astype(BF16)

    live = lax.broadcasted_iota(jnp.int32, (1, SLOTS), 1) < oc[0, 0]
    o0 = jnp.where(live, obs[0], 0.0)
    s1 = o0 / obs[1]
    obs[0] = o0
    obs[2] = s1
    terms[...] = wv[...] * s1
    gsend = [
        send(terms, terms_n, sem_gs.at[0], sem_gr.at[0], before, t),
        send(oiv, oiv_n, sem_gs.at[1], sem_gr.at[1], before, t),
    ]
    for copy in gsend:
        copy.start()
    place_slots(oiv[...], lonb, onehot)

    def pieces(x):
        high = x.astype(BF16)
        return high, (x - high.astype(F32)).astype(BF16)

    def spread(values, lons, hot):
        total = jnp.zeros((LON * LEV, LAT), F32)
        for n in range(SLOTS // CHUNK):
            cols = pl.ds(n * CHUNK, CHUNK)
            ids = lax.broadcasted_iota(jnp.int32, (LON, LEV, CHUNK), 0)
            placed = jnp.where(ids == lons[:, cols][None], values[:, cols][None], 0.0).reshape(LON * LEV, CHUNK)
            for piece in pieces(placed):
                total += lax.dot_general(piece, hot[:, cols], (((1,), (1,)), ((), ())), preferred_element_type=F32)
        return total.reshape(LON, LEV, LAT)

    def observe(field, row):
        high, low = pieces(field.reshape(LON * LEV, LAT))
        for n in range(SLOTS // CHUNK):
            cols = pl.ds(n * CHUNK, CHUNK)
            picked = jnp.dot(high, onehot[:, cols], preferred_element_type=F32)
            picked += jnp.dot(low, onehot[:, cols], preferred_element_type=F32)
            picked = picked.reshape(LON, LEV, CHUNK)
            here = lonb[:, cols]
            column = jnp.zeros((LEV, CHUNK), F32)
            for i in range(LON):
                column = jnp.where(here == i, picked[i], column)
            total = jnp.sum(column * wv[:, cols], axis=0, keepdims=True)
            slot = lax.broadcasted_iota(jnp.int32, (1, CHUNK), 1) + n * CHUNK
            obs[row, :, cols] = jnp.where(slot < oc[0, 0], total, 0.0)

    gb[...] = spread(terms, lonb, onehot)
    for lt in range(LAT // 128):
        sl = pl.ds(lt * 128, 128)
        u = gb[:, :, sl]
        for n, off in ((8, 0), (4, 8), (2, 12), (1, 14)):
            pair = u.reshape(n, 2, LEV, 128)
            hb[pl.ds(off, n), :, sl] = pair[:, 0] - pair[:, 1]
            u = pair[:, 0] + pair[:, 1]
        cu[pl.ds(place, 1), :, sl] = u
    coarse = []
    for j in range(1, 4):
        peer, back = (place + j) % 4, (place + 4 - j) % 4
        out = send(cu.at[place], cu.at[place], sem_cs.at[j], sem_cr.at[j], k, base + peer)
        out.start()
        coarse.append((out, send(cu.at[place], cu.at[back], sem_cs.at[j], sem_cr.at[j], k, base + back)))

    level_ids = lax.broadcasted_iota(jnp.int32, (LEV, LEV), 0)
    other_ids = lax.broadcasted_iota(jnp.int32, (LEV, LEV), 1)
    mixing = vmv[0] + jnp.where(level_ids == other_ids, 0.7, 0.0).astype(F32)
    for r in range(LEV):
        chosen = jnp.where(other_ids == (level_ids + r) % LEV, mixing, 0.0)
        mixf[r] = jnp.broadcast_to(jnp.sum(chosen, axis=1, keepdims=True), (LEV, LAT))
    mixb[0] = mixf[0]
    for r in range(1, LEV):
        mixb[r] = pltpu.roll(mixf[LEV - r], LEV - r, 0)
    lanes = lax.broadcasted_iota(jnp.int32, (LEV, LAT), 1)
    dn = jnp.where(lanes < LAT - 1, dfv[0], 0.0)
    dp = pltpu.roll(dn, 1, 1)
    latc[0] = dn
    latc[1] = dp
    latc[2] = 1.0 - dn - dp

    def weigh(start, count):
        cols = pl.ds(start, count)
        c = ac[1, cols]
        sq = c * c
        wts[0, cols] = (sq + c) * 0.5
        wts[1, cols] = 1.0 - sq
        wts[2, cols] = (sq - c) * 0.5

    for n in range(4):
        weigh(HALO + 4 * n, 4)

    def latitude(a):
        return latc[2] * a + latc[0] * pltpu.roll(a, LAT - 1, 2) + latc[1] * pltpu.roll(a, 1, 2)

    def couple(b, mix):
        total = mix[0] * b
        for r in range(1, LEV):
            total += mix[r] * pltpu.roll(b, LEV - r, 1)
        return total

    def forward(start, out):
        path = [(start, bufa, 0), (bufa, bufb, 0), (bufb, bufa, 0), (bufa, out, HALO)]
        for step, ((src, dst, off), blocks) in enumerate(zip(path, (6, 5, 5, 4))):

            def block(n, carry):
                i = step + 1 + 4 * n
                u = src[pl.ds(i - 1, 6)]
                a = wts[0, pl.ds(i, 4)] * u[0:4] + wts[1, pl.ds(i, 4)] * u[1:5] + wts[2, pl.ds(i, 4)] * u[2:6]
                dst[pl.ds(i - off, 4)] = couple(latitude(a), mixf)
                return carry

            lax.fori_loop(0, blocks, block, 0, unroll=True)

    def backward(start, out):
        path = [(start, bufa, 0), (bufa, bufb, 0), (bufb, bufa, 0), (bufa, out, HALO)]
        for step, ((src, dst, off), wide, narrow) in enumerate(zip(path, (6, 6, 5, 5), (6, 5, 5, 4))):

            def inner(n, carry):
                i = step + 4 * n
                bufg[pl.ds(i, 4)] = latitude(couple(src[pl.ds(i, 4)], mixb))
                return carry

            def outer(n, carry):
                i = step + 1 + 4 * n
                z = wts[1, pl.ds(i, 4)] * bufg[pl.ds(i, 4)]
                z += wts[0, pl.ds(i + 1, 4)] * bufg[pl.ds(i + 1, 4)]
                z += wts[2, pl.ds(i - 1, 4)] * bufg[pl.ds(i - 1, 4)]
                dst[pl.ds(i - off, 4)] = z
                return carry

            lax.fori_loop(0, wide, inner, 0, unroll=True)
            lax.fori_loop(0, narrow, outer, 0, unroll=True)

    for copy in halo:
        copy.wait()
    weigh(0, HALO)
    weigh(HALO + LON, HALO)
    forward(ac.at[0], mo.at[0])
    shift = send(mo.at[0], ma, sem_ts.at[0], sem_tr.at[0], later, t)
    asend = send(ac.at[0, pl.ds(HALO, LON)], an, sem_ts.at[1], sem_tr.at[1], before, t)
    shift.start()

    for out, came in first:
        came.wait_recv()
    turned = jnp.transpose(r1[...].reshape(LAT, 128))
    s2[...] = turned.reshape(SIDE, LON, LAT)
    second = []
    for j in FAR_FIRST:
        peer, back = (y + j) % SIDE, (y + SIDE - j) % SIDE
        out = send(s2.at[peer], r2.at[y], sem_2s.at[j], sem_2r.at[j], *on_y(peer))
        out.start()
        second.append((out, send(s2.at[peer], r2.at[back], sem_2s.at[j], sem_2r.at[j], *on_y(back))))
    r2[pl.ds(y, 1)] = s2[pl.ds(y, 1)]

    observe(ac[0, pl.ds(HALO, LON)], 3)
    q1 = obs[0] + obs[3]
    obs[3] = q1
    obs[4] = q1 / obs[1]

    htq[...] = spread(wv[...] * obs[4], lonb, onehot)

    for copy in gsend:
        copy.wait()
    place_slots(oiv_n[...], lonb_n, onehot_n)
    gx[pl.ds(HALO, LON)] = spread(terms_n, lonb_n, onehot_n)
    gedge = [
        send(gx.at[pl.ds(HALO, HALO)], gx.at[pl.ds(HALO + LON, HALO)], sem_hs.at[4], sem_hr.at[4], k, west),
        send(gx.at[pl.ds(LON, HALO)], gx.at[pl.ds(0, HALO)], sem_hs.at[5], sem_hr.at[5], k, east),
    ]
    for copy in gedge:
        copy.start()

    for out, came in coarse:
        came.wait_recv()
    for out, came in second:
        came.wait_recv()
    lane = lax.broadcasted_iota(jnp.int32, (LON, LAT), 1)
    for zz in range(4):
        for half in range(2):
            level = None
            for m in range(4):
                offset = (96 * (m - zz)) % LAT
                part = r2[half * 4 + m]
                moved = pltpu.roll(part, offset, 1) if offset else part
                level = moved if level is None else jnp.where(lane >= 96 * m, moved, level)
            vt[zz * 2 + half] = level
    vb[...] = jnp.swapaxes(vt[...], 0, 1)
    u = [cu[j] for j in range(4)]
    left, right = jnp.where(place < 2, u[0], u[2]), jnp.where(place < 2, u[1], u[3])
    total = (u[0] + u[1]) + jnp.where(place == 0, u[2] + u[3], -(u[2] + u[3]))
    coefficient = jnp.where(place % 2 == 0, total * (1 / 64), (left - right) * (1 / 32))
    wq[place] = coefficient * vb[0]
    wsend = []
    for j in range(1, 4):
        peer, back = (place + j) % 4, (place + 4 - j) % 4
        out = send(wq.at[place], wq.at[place], sem_ws.at[j], sem_wr.at[j], k, base + peer)
        out.start()
        wsend.append((out, send(wq.at[place], wq.at[back], sem_ws.at[j], sem_wr.at[j], k, base + back)))
    wside = [
        send(wq.at[place], wn.at[place], sem_ws.at[4], sem_wr.at[4 + place], k, (base + TILES - 1) % TILES),
        send(wq.at[place], wn.at[place], sem_ws.at[5], sem_wr.at[4 + place], k, (base + 4) % TILES),
    ]
    for copy in wside:
        copy.start()

    shift.wait()
    asend.start()
    for lt in range(LAT // 128):
        sl = pl.ds(lt * 128, 128)
        u = None
        for n, off, half in ((1, 14, 1 / 16), (2, 12, 1 / 8), (4, 8, 1 / 4), (8, 0, 1 / 2)):
            width = LON // n
            var = vb[:, :, sl].reshape(n, width, LEV, 128)[:, width // 2]
            d = hb[pl.ds(off, n), :, sl] * var * half
            u = jnp.concatenate([d, -d]) if u is None else jnp.stack([u + d, u - d], axis=1).reshape(2 * n, LEV, 128)
        dx[pl.ds(HALO, LON), :, sl] = ac[0, pl.ds(HALO, LON), :, sl] - jnp.where(k > 0, ma[:, :, sl], 0.0) - u
    edge = [
        send(dx.at[pl.ds(HALO, HALO)], dx.at[pl.ds(HALO + LON, HALO)], sem_hs.at[2], sem_hr.at[2], k, west),
        send(dx.at[pl.ds(LON, HALO)], dx.at[pl.ds(0, HALO)], sem_hs.at[3], sem_hr.at[3], k, east),
    ]
    for copy in edge:
        copy.start()
    for copy in gedge:
        copy.wait()
    backward(gx, mtg)
    observe(dx[pl.ds(HALO, LON)], 5)

    def state_part(n, acc):
        cols = pl.ds(4 * n, 4)
        g = gb[cols]
        f = g - jnp.where(k < WINDOWS - 1, mtg[cols], 0.0) + htq[cols]
        return acc[0] + jnp.sum(g * g, axis=0), acc[1] + jnp.sum(g * f, axis=0), acc[2] + jnp.sum(f * f, axis=0)

    zero = jnp.zeros((LEV, LAT), F32)
    gg, gf, ff = lax.fori_loop(0, 4, state_part, (zero, zero, zero), unroll=True)
    asend.wait()
    for out, came in wsend:
        came.wait_recv()

    @pl.when((place == 0) | (place == 3))
    def _():
        for j in range(4):
            send(wq.at[j], wn.at[j], sem_ws.at[4], sem_wr.at[4 + j], k, beside + j).wait_recv()

    for copy in edge:
        copy.wait()

    def on_tile(w, at):
        pair = jnp.where(at < 2, w[0] + w[2], w[0] - w[2])
        fine = jnp.where(at < 2, w[1], w[3])
        return pair + jnp.where(at % 2 == 0, fine, -fine)

    up[0] = jnp.where(place > 0, on_tile(wq, place - 1), on_tile(wn, 3))
    up[1] = on_tile(wq, place)
    up[2] = jnp.where(place < 3, on_tile(wq, place + 1), on_tile(wn, 0))
    for n, start, count in ((0, 0, HALO), (1, HALO, LON), (2, HALO + LON, HALO)):
        dx[pl.ds(start, count)] = dx[pl.ds(start, count)] - up[n][None]
    dd[...] = dx[pl.ds(HALO, LON)]

    def fold(x):
        x = jnp.sum(x, axis=0, keepdims=True)
        return sum(x[:, n : n + 128] for n in range(0, x.shape[1], 128))

    o0, q1 = obs[0], obs[3]
    picked = sum(jnp.dot(piece, onehot[...], preferred_element_type=F32) for piece in pieces(up[1]))
    flat = jnp.sum(picked * wv[...], axis=0, keepdims=True)
    h = q1 + obs[5] - jnp.where(live, flat, 0.0)
    sums = [fold(o0 * q1), fold(gg) + fold(q1 * q1), fold(o0 * h), fold(gf) + fold(q1 * h), fold(ff) + fold(h * h)]
    forward(dx, mo.at[1])

    def lam_part(n, acc):
        cols = pl.ds(4 * n, 4)
        a = an[cols]
        b = a - jnp.where(k < WINDOWS - 1, mo[0, cols], 0.0)
        e = b - jnp.where(k < WINDOWS - 1, mo[1, cols], 0.0)
        products = (a * b, b * b, a * e, b * e, e * e)
        return tuple(total + jnp.sum(product, axis=0) for total, product in zip(acc, products))

    acc = lax.fori_loop(0, 4, lam_part, (zero,) * 5, unroll=True)
    row = lax.broadcasted_iota(jnp.int32, (8, 128), 0)
    total = jnp.zeros((8, 128), F32)
    for n in range(5):
        total = jnp.where(row == n, sums[n] + fold(acc[n]), total)

    for stage, (me, ring, order, arr) in enumerate(((me_yc, on_yc, FAR_YC, arr1), (me_zx, on_zx, FAR_ZX, arr2))):
        count = len(order) + 1
        arr[0] = total
        for j in order:
            send(arr.at[0], arr.at[j], sem_a.at[stage, 0], sem_a.at[stage, 1], *ring((me + j) % count)).start()
        others = arr.at[pl.ds(1, count - 1)]
        send(others, others, sem_a.at[stage, 0], sem_a.at[stage, 1], *ring((me + 1) % count)).wait_recv()
        total = jnp.sum(arr[...], axis=0)
    total = jnp.sum(total, axis=1, keepdims=True)
    rq, qq, re, qe, ee = (total[n : n + 1] for n in range(5))
    alpha = rq / (qq + 1e-6)
    beta = alpha * (1e-6 - re + alpha * qe) / (qq - 2.0 * alpha * qe + alpha * alpha * ee + 1e-6)
    row = lax.broadcasted_iota(jnp.int32, (8, 128), 0)
    al[...] = jnp.where(row == 0, alpha, beta)
    ao[...] = ac[0, pl.ds(HALO, LON)]
    so[0] = obs[2]
    so[1] = obs[4]

    for out, came in first + second + coarse + wsend:
        out.wait_send()
    for copy in wside:
        copy.wait_send()
    for stage, (ring, arr) in enumerate(((on_yc, arr1), (on_zx, arr2))):
        others = arr.at[pl.ds(1, arr.shape[0] - 1)]
        send(others, others, sem_a.at[stage, 0], sem_a.at[stage, 1], *ring(0)).wait_send()


def finish(gb, dd, ao, so, al, mult, omult, incr):
    alpha, beta = al[0:1, 0:1], al[1:2, 0:1]
    both, cross = alpha + beta, alpha * beta
    wide_both, wide_cross = jnp.broadcast_to(both, (LEV, LAT)), jnp.broadcast_to(cross, (LEV, LAT))
    mult[0] = -wide_cross * gb[...]
    incr[0] = wide_both * ao[...] - wide_cross * dd[...]
    omult[...] = both * so[0] - cross * so[1]


def field(*lead):
    return pltpu.VMEM((*lead, LEV, LAT), F32)


SCRATCH = [
    field(2, WIDE),
    field(3, WIDE),
    pltpu.VMEM((LAT, SLOTS), BF16),
    pltpu.VMEM((LAT, SLOTS), BF16),
    pltpu.VMEM((LEV, SLOTS), jnp.int32),
    pltpu.VMEM((LEV, SLOTS), jnp.int32),
    pltpu.VMEM((6, 1, SLOTS), F32),
    pltpu.VMEM((1, SLOTS), jnp.int32),
    pltpu.VMEM((1, SLOTS), jnp.int32),
    pltpu.VMEM((LEV, SLOTS), F32),
    pltpu.VMEM((LEV, SLOTS), F32),
    pltpu.VMEM((LEV, SLOTS), F32),
    field(1),
    pltpu.VMEM((1, LEV, LEV), F32),
    field(3),
    field(LEV),
    field(LEV),
    field(WIDE),
    field(WIDE),
    field(WIDE),
    field(WIDE),
    field(2, LON),
    field(LON),
    field(LON),
    field(LON),
    field(LON),
    field(WIDE),
    field(LON),
    field(4),
    pltpu.VMEM((LAT // SIDE, TILES * LON), F32),
    pltpu.VMEM((SIDE, LAT // SIDE, 128), F32),
    pltpu.VMEM((SIDE, LAT // SIDE, 128), F32),
    pltpu.VMEM((SIDE, LON, LAT), F32),
    pltpu.VMEM((SIDE, LON, LAT), F32),
    pltpu.VMEM((LEV, LON, LAT), F32),
    field(LON),
    field(4),
    field(4),
    field(3),
    pltpu.VMEM((16, 8, 128), F32),
    pltpu.VMEM((32, 8, 128), F32),
] + [
    pltpu.SemaphoreType.DMA(shape)
    for shape in (
        (9,), (6,), (6,), (8,), (8,), (8,), (8,), (8,), (8,), (4,), (4,), (2,), (2,), (2,), (2,), (2, 2),
    )
]


def body(md, od, ov, ow, oi, oc, cr, df, vm, ev):
    inputs = (md[0], od, ov, ow[0], oi, oc, cr[0], df, vm, jnp.swapaxes(ev[0], 0, 1))
    inputs = [x if x is oc else pltpu.with_memory_space_constraint(x, pltpu.HBM) for x in inputs]
    hbm = [pl.BlockSpec(memory_space=pltpu.HBM)]
    vmem = pl.BlockSpec(memory_space=pltpu.VMEM)
    plane = jax.ShapeDtypeStruct((LON, LEV, LAT), F32)
    parts = pl.pallas_call(
        kernel,
        out_shape=(plane, plane, plane, jax.ShapeDtypeStruct((2, 1, SLOTS), F32), jax.ShapeDtypeStruct((8, 128), F32)),
        in_specs=hbm * 5 + [pl.BlockSpec(memory_space=pltpu.SMEM)] + hbm * 4,
        out_specs=(vmem,) * 5,
        scratch_shapes=SCRATCH,
        compiler_params=pltpu.CompilerParams(
            collective_id=0, has_side_effects=True, vmem_limit_bytes=40 * 1024 * 1024
        ),
        name="saddle",
    )(*inputs)
    return pl.pallas_call(
        finish,
        out_shape=(
            jax.ShapeDtypeStruct((1, LON, LEV, LAT), F32),
            jax.ShapeDtypeStruct((1, SLOTS), F32),
            jax.ShapeDtypeStruct((1, LON, LEV, LAT), F32),
        ),
        compiler_params=pltpu.CompilerParams(vmem_limit_bytes=8 * 1024 * 1024),
        name="finish",
    )(*parts)


def solution(mesh):
    in_specs = (
        P("tm", "space", None, None),
        P("tm", "space"),
        P("tm", "space"),
        P("tm", None, "space"),
        P("tm", "space"),
        P("tm", "space"),
        P("tm", "space", None, None),
        P("tm", None, None),
        P("tm", None, None),
        P("tm", None, "space"),
    )
    out_specs = (P("tm", "space", None, None), P("tm", "space"), P("tm", "space", None, None))
    return jax.shard_map(body, mesh=mesh, in_specs=in_specs, out_specs=out_specs, check_vma=False)
```

```python
import jax
import jax.numpy as jnp
from jax import lax
from jax.experimental import pallas as pl
from jax.experimental.pallas import tpu as pltpu
from jax.sharding import PartitionSpec as P

MESH = pl.DeviceIdType.MESH
F32 = jnp.float32
BF16 = jnp.bfloat16
LON, LEV, LAT, SLOTS = 16, 8, 384, 2048
WINDOWS, TILES, SIDE = 8, 64, 8
HALO = 4
WIDE = LON + 2 * HALO + 2
CHUNK = 512
FAR_FIRST = (4, 3, 5, 2, 6, 1, 7)
FAR_YC = (8, 7, 9, 6, 10, 5, 11, 4, 12, 3, 13, 2, 14, 1, 15)
FAR_ZX = tuple(sorted(range(1, 32), key=lambda j: (-min(j // 4, 8 - j // 4), j)))


def kernel(
    md, od, ov, ow, oi, oc, cr, df, vm, ev,
    gb, dd, ao, so, al,
    ac, wts, onehot, onehot_n, lonb, lonb_n, obs, oiv, oiv_n, wv, terms, terms_n, dfv, vmv, latc, mixf, mixb,
    gx, bufa, bufb, bufg, mo, ma, an, mtg, htq, dx,
    hb, cu, evv, evp, r1, s2, r2, vt, vb, wq, wn, up, arr1, arr2,
    sem_load, sem_hs, sem_hr, sem_1s, sem_1r, sem_2s, sem_2r, sem_ws, sem_wr, sem_cs, sem_cr, sem_gs, sem_gr, sem_ts, sem_tr, sem_a, sem_in,
):
    k = lax.axis_index("tm")
    t = lax.axis_index("space")
    x, zl = k // 2, k % 2
    zh, y, c = t // 16, t // 2 % 8, t % 2
    east, west = (t + 1) % TILES, (t + TILES - 1) % TILES
    later, before = (k + 1) % WINDOWS, (k + WINDOWS - 1) % WINDOWS
    place = t % 4
    base = t - place

    def send(src, dst, ssem, rsem, kk, tt):
        return pltpu.make_async_remote_copy(
            src_ref=src, dst_ref=dst, send_sem=ssem, recv_sem=rsem, device_id=(kk, tt), device_id_type=MESH
        )

    def tile_at(zz, yy, cc):
        return zz * 16 + yy * 2 + cc

    def on_y(place):
        return k, tile_at(zh, place, c)

    def on_zc(place):
        return k, tile_at(place // 2, y, place % 2)

    def on_yc(place):
        return k, tile_at(zh, place // 2, place % 2)

    def on_zx(place):
        return place % 4 * 2 + place // 4 % 2, tile_at(place // 8, y, c)

    loads = [
        pltpu.make_async_copy(src, dst, sem_load.at[n])
        for n, (src, dst) in enumerate(
            [
                (ev, evv),
                (md, ac.at[0, pl.ds(HALO, LON)]),
                (cr, ac.at[1, pl.ds(HALO, LON)]),
                (oi, oiv),
                (od, obs.at[0]),
                (ov, obs.at[1]),
                (ow, wv),
                (df, dfv),
                (vm, vmv),
            ]
        )
    ]
    for load in loads:
        load.start()

    barrier = pltpu.get_barrier_semaphore()

    def greet(kk, tt):
        pl.semaphore_signal(barrier, inc=1, device_id=(kk, tt), device_id_type=MESH)

    me_yc, me_zx = y * 2 + c, (zh * 2 + zl) * 4 + x
    for j in FAR_YC:
        greet(*on_yc((me_yc + j) % 16))
    for j in FAR_FIRST:
        greet(*on_zx((me_zx + 4 * j) % 32))
    for j in range(1, 4):
        greet(k, tile_at((zh + j) % 4, y, 1 - c))
        greet((x + j) % 4 * 2 + zl, t)
    greet(later, t)
    greet(before, t)
    greet(k, east)
    greet(k, west)
    beside = jnp.where(place == 0, base + TILES - 4, base + 4) % TILES

    @pl.when((place == 0) | (place == 3))
    def _():
        for j in range(4):
            greet(k, beside + j)


    lane_v = lax.broadcasted_iota(jnp.int32, (LAT // SIDE, 128), 1)
    loads[0].wait()
    for zz in range(4):
        for cc in range(2):
            block = None
            for yy in range(SIDE):
                source = evv[:, pl.ds((zz * 2 + yy // 4) * 128, 128)]
                offset = (yy * 16 - (yy % 4 * 32 + cc * 16)) % 128
                moved = pltpu.roll(source, offset, 1) if offset else source
                block = moved if block is None else jnp.where(lane_v >= yy * 16, moved, block)
            evp[zz * 2 + cc] = block
    halo = [
        send(ac.at[:, pl.ds(HALO, HALO)], ac.at[:, pl.ds(HALO + LON, HALO)], sem_hs.at[0], sem_hr.at[0], k, west),
        send(ac.at[:, pl.ds(LON, HALO)], ac.at[:, pl.ds(0, HALO)], sem_hs.at[1], sem_hr.at[1], k, east),
    ]
    loads[1].wait()
    loads[2].wait()
    pl.semaphore_wait(barrier, 34)
    for copy in halo:
        copy.start()

    me = zh * 2 + c
    first = []
    for j in FAR_FIRST:
        peer, back = (me + j) % SIDE, (me + SIDE - j) % SIDE
        out = send(evp.at[peer], r1.at[me], sem_1s.at[j], sem_1r.at[j], *on_zc(peer))
        out.start()
        first.append((out, send(evp.at[peer], r1.at[back], sem_1s.at[j], sem_1r.at[j], *on_zc(back))))
    r1[pl.ds(me, 1)] = evp[pl.ds(me, 1)]

    for j in FAR_FIRST:
        kk, tt = on_zx((me_zx + 4 * j) % 32)
        pl.semaphore_signal(sem_in, inc=1, device_id=(kk, tt), device_id_type=MESH)

    for load in loads[3:]:
        load.wait()

    def place_slots(index, lon_out, hot_out):
        lon = (index * 10923) >> 22
        lat = index - lon * LAT
        lon_out[...] = jnp.broadcast_to(lon, (LEV, SLOTS))
        for n in range(SLOTS // CHUNK):
            rows = lax.broadcasted_iota(jnp.int32, (LAT, CHUNK), 0)
            hot = jnp.where(rows == lat[:, n * CHUNK : (n + 1) * CHUNK], 1.0, 0.0)
            hot_out[:, pl.ds(n * CHUNK, CHUNK)] = hot.astype(BF16)

    live = lax.broadcasted_iota(jnp.int32, (1, SLOTS), 1) < oc[0, 0]
    o0 = jnp.where(live, obs[0], 0.0)
    s1 = o0 / obs[1]
    obs[0] = o0
    obs[2] = s1
    terms[...] = wv[...] * s1
    gsend = [
        send(terms, terms_n, sem_gs.at[0], sem_gr.at[0], before, t),
        send(oiv, oiv_n, sem_gs.at[1], sem_gr.at[1], before, t),
    ]
    for copy in gsend:
        copy.start()
    place_slots(oiv[...], lonb, onehot)

    def pieces(x):
        high = x.astype(BF16)
        return high, (x - high.astype(F32)).astype(BF16)

    def spread(values, lons, hot):
        total = jnp.zeros((LON * LEV, LAT), F32)
        for n in range(SLOTS // CHUNK):
            cols = pl.ds(n * CHUNK, CHUNK)
            ids = lax.broadcasted_iota(jnp.int32, (LON, LEV, CHUNK), 0)
            placed = jnp.where(ids == lons[:, cols][None], values[:, cols][None], 0.0).reshape(LON * LEV, CHUNK)
            for piece in pieces(placed):
                total += lax.dot_general(piece, hot[:, cols], (((1,), (1,)), ((), ())), preferred_element_type=F32)
        return total.reshape(LON, LEV, LAT)

    def observe(field, row):
        high, low = pieces(field.reshape(LON * LEV, LAT))
        for n in range(SLOTS // CHUNK):
            cols = pl.ds(n * CHUNK, CHUNK)
            picked = jnp.dot(high, onehot[:, cols], preferred_element_type=F32)
            picked += jnp.dot(low, onehot[:, cols], preferred_element_type=F32)
            picked = picked.reshape(LON, LEV, CHUNK)
            here = lonb[:, cols]
            column = jnp.zeros((LEV, CHUNK), F32)
            for i in range(LON):
                column = jnp.where(here == i, picked[i], column)
            total = jnp.sum(column * wv[:, cols], axis=0, keepdims=True)
            slot = lax.broadcasted_iota(jnp.int32, (1, CHUNK), 1) + n * CHUNK
            obs[row, :, cols] = jnp.where(slot < oc[0, 0], total, 0.0)

    gb[...] = spread(terms, lonb, onehot)
    for lt in range(LAT // 128):
        sl = pl.ds(lt * 128, 128)
        u = gb[:, :, sl]
        for n, off in ((8, 0), (4, 8), (2, 12), (1, 14)):
            pair = u.reshape(n, 2, LEV, 128)
            hb[pl.ds(off, n), :, sl] = pair[:, 0] - pair[:, 1]
            u = pair[:, 0] + pair[:, 1]
        cu[pl.ds(place, 1), :, sl] = u
    coarse = []
    for j in range(1, 4):
        peer, back = (place + j) % 4, (place + 4 - j) % 4
        out = send(cu.at[place], cu.at[place], sem_cs.at[j], sem_cr.at[j], k, base + peer)
        out.start()
        coarse.append((out, send(cu.at[place], cu.at[back], sem_cs.at[j], sem_cr.at[j], k, base + back)))

    level_ids = lax.broadcasted_iota(jnp.int32, (LEV, LEV), 0)
    other_ids = lax.broadcasted_iota(jnp.int32, (LEV, LEV), 1)
    mixing = vmv[0] + jnp.where(level_ids == other_ids, 0.7, 0.0).astype(F32)
    for r in range(LEV):
        chosen = jnp.where(other_ids == (level_ids + r) % LEV, mixing, 0.0)
        mixf[r] = jnp.broadcast_to(jnp.sum(chosen, axis=1, keepdims=True), (LEV, LAT))
    mixb[0] = mixf[0]
    for r in range(1, LEV):
        mixb[r] = pltpu.roll(mixf[LEV - r], LEV - r, 0)
    lanes = lax.broadcasted_iota(jnp.int32, (LEV, LAT), 1)
    dn = jnp.where(lanes < LAT - 1, dfv[0], 0.0)
    dp = pltpu.roll(dn, 1, 1)
    latc[0] = dn
    latc[1] = dp
    latc[2] = 1.0 - dn - dp

    def weigh(start, count):
        cols = pl.ds(start, count)
        c = ac[1, cols]
        sq = c * c
        wts[0, cols] = (sq + c) * 0.5
        wts[1, cols] = 1.0 - sq
        wts[2, cols] = (sq - c) * 0.5

    for n in range(4):
        weigh(HALO + 4 * n, 4)

    def latitude(a):
        return latc[2] * a + latc[0] * pltpu.roll(a, LAT - 1, 2) + latc[1] * pltpu.roll(a, 1, 2)

    def couple(b, mix):
        total = mix[0] * b
        for r in range(1, LEV):
            total += mix[r] * pltpu.roll(b, LEV - r, 1)
        return total

    def forward(start, out):
        path = [(start, bufa, 0), (bufa, bufb, 0), (bufb, bufa, 0), (bufa, out, HALO)]
        for step, ((src, dst, off), blocks) in enumerate(zip(path, (6, 5, 5, 4))):

            def block(n, carry):
                i = step + 1 + 4 * n
                u = src[pl.ds(i - 1, 6)]
                a = wts[0, pl.ds(i, 4)] * u[0:4] + wts[1, pl.ds(i, 4)] * u[1:5] + wts[2, pl.ds(i, 4)] * u[2:6]
                dst[pl.ds(i - off, 4)] = couple(latitude(a), mixf)
                return carry

            lax.fori_loop(0, blocks, block, 0, unroll=True)

    def backward(start, out):
        path = [(start, bufa, 0), (bufa, bufb, 0), (bufb, bufa, 0), (bufa, out, HALO)]
        for step, ((src, dst, off), wide, narrow) in enumerate(zip(path, (6, 6, 5, 5), (6, 5, 5, 4))):

            def inner(n, carry):
                i = step + 4 * n
                bufg[pl.ds(i, 4)] = latitude(couple(src[pl.ds(i, 4)], mixb))
                return carry

            def outer(n, carry):
                i = step + 1 + 4 * n
                z = wts[1, pl.ds(i, 4)] * bufg[pl.ds(i, 4)]
                z += wts[0, pl.ds(i + 1, 4)] * bufg[pl.ds(i + 1, 4)]
                z += wts[2, pl.ds(i - 1, 4)] * bufg[pl.ds(i - 1, 4)]
                dst[pl.ds(i - off, 4)] = z
                return carry

            lax.fori_loop(0, wide, inner, 0, unroll=True)
            lax.fori_loop(0, narrow, outer, 0, unroll=True)

    for copy in halo:
        copy.wait()
    weigh(0, HALO)
    weigh(HALO + LON, HALO)
    forward(ac.at[0], mo.at[0])
    shift = send(mo.at[0], ma, sem_ts.at[0], sem_tr.at[0], later, t)
    asend = send(ac.at[0, pl.ds(HALO, LON)], an, sem_ts.at[1], sem_tr.at[1], before, t)
    shift.start()
    asend.start()

    for out, came in first:
        came.wait_recv()
    turned = jnp.transpose(r1[...].reshape(LAT, 128))
    s2[...] = turned.reshape(SIDE, LON, LAT)
    second = []
    for j in FAR_FIRST:
        peer, back = (y + j) % SIDE, (y + SIDE - j) % SIDE
        out = send(s2.at[peer], r2.at[y], sem_2s.at[j], sem_2r.at[j], *on_y(peer))
        out.start()
        second.append((out, send(s2.at[peer], r2.at[back], sem_2s.at[j], sem_2r.at[j], *on_y(back))))
    r2[pl.ds(y, 1)] = s2[pl.ds(y, 1)]

    observe(ac[0, pl.ds(HALO, LON)], 3)
    q1 = obs[0] + obs[3]
    obs[3] = q1
    obs[4] = q1 / obs[1]

    htq[...] = spread(wv[...] * obs[4], lonb, onehot)

    for copy in gsend:
        copy.wait()
    place_slots(oiv_n[...], lonb_n, onehot_n)
    gx[pl.ds(HALO, LON)] = spread(terms_n, lonb_n, onehot_n)
    gedge = [
        send(gx.at[pl.ds(HALO, HALO)], gx.at[pl.ds(HALO + LON, HALO)], sem_hs.at[4], sem_hr.at[4], k, west),
        send(gx.at[pl.ds(LON, HALO)], gx.at[pl.ds(0, HALO)], sem_hs.at[5], sem_hr.at[5], k, east),
    ]
    for copy in gedge:
        copy.start()

    for out, came in coarse:
        came.wait_recv()
    for out, came in second:
        came.wait_recv()
    lane = lax.broadcasted_iota(jnp.int32, (LON, LAT), 1)
    for zz in range(4):
        for half in range(2):
            level = None
            for m in range(4):
                offset = (96 * (m - zz)) % LAT
                part = r2[half * 4 + m]
                moved = pltpu.roll(part, offset, 1) if offset else part
                level = moved if level is None else jnp.where(lane >= 96 * m, moved, level)
            vt[zz * 2 + half] = level
    vb[...] = jnp.swapaxes(vt[...], 0, 1)
    u = [cu[j] for j in range(4)]
    left, right = jnp.where(place < 2, u[0], u[2]), jnp.where(place < 2, u[1], u[3])
    total = (u[0] + u[1]) + jnp.where(place == 0, u[2] + u[3], -(u[2] + u[3]))
    coefficient = jnp.where(place % 2 == 0, total * (1 / 64), (left - right) * (1 / 32))
    wq[place] = coefficient * vb[0]
    wsend = []
    for j in range(1, 4):
        peer, back = (place + j) % 4, (place + 4 - j) % 4
        out = send(wq.at[place], wq.at[place], sem_ws.at[j], sem_wr.at[j], k, base + peer)
        out.start()
        wsend.append((out, send(wq.at[place], wq.at[back], sem_ws.at[j], sem_wr.at[j], k, base + back)))
    wside = [
        send(wq.at[place], wn.at[place], sem_ws.at[4], sem_wr.at[4 + place], k, (base + TILES - 1) % TILES),
        send(wq.at[place], wn.at[place], sem_ws.at[5], sem_wr.at[4 + place], k, (base + 4) % TILES),
    ]
    for copy in wside:
        copy.start()

    shift.wait()
    for lt in range(LAT // 128):
        sl = pl.ds(lt * 128, 128)
        u = None
        for n, off, half in ((1, 14, 1 / 16), (2, 12, 1 / 8), (4, 8, 1 / 4), (8, 0, 1 / 2)):
            width = LON // n
            var = vb[:, :, sl].reshape(n, width, LEV, 128)[:, width // 2]
            d = hb[pl.ds(off, n), :, sl] * var * half
            u = jnp.concatenate([d, -d]) if u is None else jnp.stack([u + d, u - d], axis=1).reshape(2 * n, LEV, 128)
        dx[pl.ds(HALO, LON), :, sl] = ac[0, pl.ds(HALO, LON), :, sl] - jnp.where(k > 0, ma[:, :, sl], 0.0) - u
    edge = [
        send(dx.at[pl.ds(HALO, HALO)], dx.at[pl.ds(HALO + LON, HALO)], sem_hs.at[2], sem_hr.at[2], k, west),
        send(dx.at[pl.ds(LON, HALO)], dx.at[pl.ds(0, HALO)], sem_hs.at[3], sem_hr.at[3], k, east),
    ]
    for copy in edge:
        copy.start()
    for copy in gedge:
        copy.wait()
    backward(gx, mtg)
    observe(dx[pl.ds(HALO, LON)], 5)

    def state_part(n, acc):
        cols = pl.ds(4 * n, 4)
        g = gb[cols]
        f = g - jnp.where(k < WINDOWS - 1, mtg[cols], 0.0) + htq[cols]
        return acc[0] + jnp.sum(g * g, axis=0), acc[1] + jnp.sum(g * f, axis=0), acc[2] + jnp.sum(f * f, axis=0)

    zero = jnp.zeros((LEV, LAT), F32)
    gg, gf, ff = lax.fori_loop(0, 4, state_part, (zero, zero, zero), unroll=True)
    for out, came in wsend:
        came.wait_recv()

    @pl.when((place == 0) | (place == 3))
    def _():
        for j in range(4):
            send(wq.at[j], wn.at[j], sem_ws.at[4], sem_wr.at[4 + j], k, beside + j).wait_recv()

    for copy in edge:
        copy.wait()

    def on_tile(w, at):
        pair = jnp.where(at < 2, w[0] + w[2], w[0] - w[2])
        fine = jnp.where(at < 2, w[1], w[3])
        return pair + jnp.where(at % 2 == 0, fine, -fine)

    up[0] = jnp.where(place > 0, on_tile(wq, place - 1), on_tile(wn, 3))
    up[1] = on_tile(wq, place)
    up[2] = jnp.where(place < 3, on_tile(wq, place + 1), on_tile(wn, 0))
    for n, start, count in ((0, 0, HALO), (1, HALO, LON), (2, HALO + LON, HALO)):
        dx[pl.ds(start, count)] = dx[pl.ds(start, count)] - up[n][None]
    dd[...] = dx[pl.ds(HALO, LON)]

    def fold(x):
        x = jnp.sum(x, axis=0, keepdims=True)
        return sum(x[:, n : n + 128] for n in range(0, x.shape[1], 128))

    o0, q1 = obs[0], obs[3]
    picked = sum(jnp.dot(piece, onehot[...], preferred_element_type=F32) for piece in pieces(up[1]))
    flat = jnp.sum(picked * wv[...], axis=0, keepdims=True)
    h = q1 + obs[5] - jnp.where(live, flat, 0.0)
    sums = [fold(o0 * q1), fold(gg) + fold(q1 * q1), fold(o0 * h), fold(gf) + fold(q1 * h), fold(ff) + fold(h * h)]
    forward(dx, mo.at[1])

    asend.wait()

    def lam_part(n, acc):
        cols = pl.ds(4 * n, 4)
        a = an[cols]
        b = a - jnp.where(k < WINDOWS - 1, mo[0, cols], 0.0)
        e = b - jnp.where(k < WINDOWS - 1, mo[1, cols], 0.0)
        products = (a * b, b * b, a * e, b * e, e * e)
        return tuple(total + jnp.sum(product, axis=0) for total, product in zip(acc, products))

    acc = lax.fori_loop(0, 4, lam_part, (zero,) * 5, unroll=True)
    row = lax.broadcasted_iota(jnp.int32, (8, 128), 0)
    total = jnp.zeros((8, 128), F32)
    for n in range(5):
        total = jnp.where(row == n, sums[n] + fold(acc[n]), total)

    for stage, (me, ring, order, arr) in enumerate(((me_yc, on_yc, FAR_YC, arr1), (me_zx, on_zx, FAR_ZX, arr2))):
        count = len(order) + 1
        if stage == 1:
            pl.semaphore_wait(sem_in, SIDE - 1)
        arr[0] = total
        for j in order:
            send(arr.at[0], arr.at[j], sem_a.at[stage, 0], sem_a.at[stage, 1], *ring((me + j) % count)).start()
        others = arr.at[pl.ds(1, count - 1)]
        send(others, others, sem_a.at[stage, 0], sem_a.at[stage, 1], *ring((me + 1) % count)).wait_recv()
        total = jnp.sum(arr[...], axis=0)
    total = jnp.sum(total, axis=1, keepdims=True)
    rq, qq, re, qe, ee = (total[n : n + 1] for n in range(5))
    alpha = rq / (qq + 1e-6)
    beta = alpha * (1e-6 - re + alpha * qe) / (qq - 2.0 * alpha * qe + alpha * alpha * ee + 1e-6)
    row = lax.broadcasted_iota(jnp.int32, (8, 128), 0)
    al[...] = jnp.where(row == 0, alpha, beta)
    ao[...] = ac[0, pl.ds(HALO, LON)]
    so[0] = obs[2]
    so[1] = obs[4]

    for out, came in first + second + coarse + wsend:
        out.wait_send()
    for copy in wside:
        copy.wait_send()
    for stage, (ring, arr) in enumerate(((on_yc, arr1), (on_zx, arr2))):
        others = arr.at[pl.ds(1, arr.shape[0] - 1)]
        send(others, others, sem_a.at[stage, 0], sem_a.at[stage, 1], *ring(0)).wait_send()


def finish(gb, dd, ao, so, al, mult, omult, incr):
    alpha, beta = al[0:1, 0:1], al[1:2, 0:1]
    both, cross = alpha + beta, alpha * beta
    wide_both, wide_cross = jnp.broadcast_to(both, (LEV, LAT)), jnp.broadcast_to(cross, (LEV, LAT))
    mult[0] = -wide_cross * gb[...]
    incr[0] = wide_both * ao[...] - wide_cross * dd[...]
    omult[...] = both * so[0] - cross * so[1]


def field(*lead):
    return pltpu.VMEM((*lead, LEV, LAT), F32)


SCRATCH = [
    field(2, WIDE),
    field(3, WIDE),
    pltpu.VMEM((LAT, SLOTS), BF16),
    pltpu.VMEM((LAT, SLOTS), BF16),
    pltpu.VMEM((LEV, SLOTS), jnp.int32),
    pltpu.VMEM((LEV, SLOTS), jnp.int32),
    pltpu.VMEM((6, 1, SLOTS), F32),
    pltpu.VMEM((1, SLOTS), jnp.int32),
    pltpu.VMEM((1, SLOTS), jnp.int32),
    pltpu.VMEM((LEV, SLOTS), F32),
    pltpu.VMEM((LEV, SLOTS), F32),
    pltpu.VMEM((LEV, SLOTS), F32),
    field(1),
    pltpu.VMEM((1, LEV, LEV), F32),
    field(3),
    field(LEV),
    field(LEV),
    field(WIDE),
    field(WIDE),
    field(WIDE),
    field(WIDE),
    field(2, LON),
    field(LON),
    field(LON),
    field(LON),
    field(LON),
    field(WIDE),
    field(LON),
    field(4),
    pltpu.VMEM((LAT // SIDE, TILES * LON), F32),
    pltpu.VMEM((SIDE, LAT // SIDE, 128), F32),
    pltpu.VMEM((SIDE, LAT // SIDE, 128), F32),
    pltpu.VMEM((SIDE, LON, LAT), F32),
    pltpu.VMEM((SIDE, LON, LAT), F32),
    pltpu.VMEM((LEV, LON, LAT), F32),
    field(LON),
    field(4),
    field(4),
    field(3),
    pltpu.VMEM((16, 8, 128), F32),
    pltpu.VMEM((32, 8, 128), F32),
] + [
    pltpu.SemaphoreType.DMA(shape)
    for shape in (
        (9,), (6,), (6,), (8,), (8,), (8,), (8,), (8,), (8,), (4,), (4,), (2,), (2,), (2,), (2,), (2, 2),
    )
] + [pltpu.SemaphoreType.REGULAR]


def body(md, od, ov, ow, oi, oc, cr, df, vm, ev):
    inputs = (md[0], od, ov, ow[0], oi, oc, cr[0], df, vm, jnp.swapaxes(ev[0], 0, 1))
    inputs = [x if x is oc else pltpu.with_memory_space_constraint(x, pltpu.HBM) for x in inputs]
    hbm = [pl.BlockSpec(memory_space=pltpu.HBM)]
    vmem = pl.BlockSpec(memory_space=pltpu.VMEM)
    plane = jax.ShapeDtypeStruct((LON, LEV, LAT), F32)
    parts = pl.pallas_call(
        kernel,
        out_shape=(plane, plane, plane, jax.ShapeDtypeStruct((2, 1, SLOTS), F32), jax.ShapeDtypeStruct((8, 128), F32)),
        in_specs=hbm * 5 + [pl.BlockSpec(memory_space=pltpu.SMEM)] + hbm * 4,
        out_specs=(vmem,) * 5,
        scratch_shapes=SCRATCH,
        compiler_params=pltpu.CompilerParams(
            collective_id=0, has_side_effects=True, vmem_limit_bytes=40 * 1024 * 1024
        ),
        name="saddle",
    )(*inputs)
    return pl.pallas_call(
        finish,
        out_shape=(
            jax.ShapeDtypeStruct((1, LON, LEV, LAT), F32),
            jax.ShapeDtypeStruct((1, SLOTS), F32),
            jax.ShapeDtypeStruct((1, LON, LEV, LAT), F32),
        ),
        compiler_params=pltpu.CompilerParams(vmem_limit_bytes=8 * 1024 * 1024),
        name="finish",
    )(*parts)


def solution(mesh):
    in_specs = (
        P("tm", "space", None, None),
        P("tm", "space"),
        P("tm", "space"),
        P("tm", None, "space"),
        P("tm", "space"),
        P("tm", "space"),
        P("tm", "space", None, None),
        P("tm", None, None),
        P("tm", None, None),
        P("tm", None, "space"),
    )
    out_specs = (P("tm", "space", None, None), P("tm", "space"), P("tm", "space", None, None))
    return jax.shard_map(body, mesh=mesh, in_specs=in_specs, out_specs=out_specs, check_vma=False)
```

```python
import jax
import jax.numpy as jnp
from jax import lax
from jax.experimental import pallas as pl
from jax.experimental.pallas import tpu as pltpu
from jax.sharding import PartitionSpec as P

MESH = pl.DeviceIdType.MESH
F32 = jnp.float32
BF16 = jnp.bfloat16
LON, LEV, LAT, SLOTS = 16, 8, 384, 2048
WINDOWS, TILES, SIDE = 8, 64, 8
HALO = 4
WIDE = LON + 2 * HALO + 2
CHUNK = 512
FAR_FIRST = (4, 3, 5, 2, 6, 1, 7)
FAR_YC = (8, 7, 9, 6, 10, 5, 11, 4, 12, 3, 13, 2, 14, 1, 15)
FAR_ZX = tuple(sorted(range(1, 32), key=lambda j: (-min(j // 4, 8 - j // 4), j)))


def kernel(
    md, od, ov, ow, oi, oc, cr, df, vm, ev,
    gb, dd, ao, so, al,
    ac, wts, onehot, onehot_n, lonb, lonb_n, obs, oiv, oiv_n, wv, terms, terms_n, dfv, vmv, latc, mixf, mixb,
    gx, bufa, bufb, bufg, mo, ma, an, mtg, htq, dx,
    hb, cu, evv, evp, r1, s2, r2, vt, vb, wq, wn, up, arr1, arr2,
    sem_load, sem_hs, sem_hr, sem_1s, sem_1r, sem_2s, sem_2r, sem_ws, sem_wr, sem_cs, sem_cr, sem_gs, sem_gr, sem_ts, sem_tr, sem_a, sem_in,
):
    k = lax.axis_index("tm")
    t = lax.axis_index("space")
    x, zl = k // 2, k % 2
    zh, y, c = t // 16, t // 2 % 8, t % 2
    east, west = (t + 1) % TILES, (t + TILES - 1) % TILES
    later, before = (k + 1) % WINDOWS, (k + WINDOWS - 1) % WINDOWS
    place = t % 4
    base = t - place

    def send(src, dst, ssem, rsem, kk, tt):
        return pltpu.make_async_remote_copy(
            src_ref=src, dst_ref=dst, send_sem=ssem, recv_sem=rsem, device_id=(kk, tt), device_id_type=MESH
        )

    def tile_at(zz, yy, cc):
        return zz * 16 + yy * 2 + cc

    def on_y(place):
        return k, tile_at(zh, place, c)

    def on_zc(place):
        return k, tile_at(place // 2, y, place % 2)

    def on_yc(place):
        return k, tile_at(zh, place // 2, place % 2)

    def on_zx(place):
        return place % 4 * 2 + place // 4 % 2, tile_at(place // 8, y, c)

    barrier = pltpu.get_barrier_semaphore()

    def greet(kk, tt):
        pl.semaphore_signal(barrier, inc=1, device_id=(kk, tt), device_id_type=MESH)

    me_yc, me_zx = y * 2 + c, (zh * 2 + zl) * 4 + x
    for j in FAR_YC:
        greet(*on_yc((me_yc + j) % 16))
    for j in FAR_FIRST:
        greet(*on_zx((me_zx + 4 * j) % 32))
    for j in range(1, 4):
        greet(k, tile_at((zh + j) % 4, y, 1 - c))
        greet((x + j) % 4 * 2 + zl, t)
    greet(later, t)
    greet(before, t)
    greet(k, east)
    greet(k, west)
    beside = jnp.where(place == 0, base + TILES - 4, base + 4) % TILES

    @pl.when((place == 0) | (place == 3))
    def _():
        for j in range(4):
            greet(k, beside + j)


    loads = [
        pltpu.make_async_copy(src, dst, sem_load.at[n])
        for n, (src, dst) in enumerate(
            [
                (ev, evv),
                (md, ac.at[0, pl.ds(HALO, LON)]),
                (cr, ac.at[1, pl.ds(HALO, LON)]),
                (oi, oiv),
                (od, obs.at[0]),
                (ov, obs.at[1]),
                (ow, wv),
                (df, dfv),
                (vm, vmv),
            ]
        )
    ]
    for load in loads:
        load.start()

    lane_v = lax.broadcasted_iota(jnp.int32, (LAT // SIDE, 128), 1)
    loads[0].wait()
    for zz in range(4):
        for cc in range(2):
            block = None
            for yy in range(SIDE):
                source = evv[:, pl.ds((zz * 2 + yy // 4) * 128, 128)]
                offset = (yy * 16 - (yy % 4 * 32 + cc * 16)) % 128
                moved = pltpu.roll(source, offset, 1) if offset else source
                block = moved if block is None else jnp.where(lane_v >= yy * 16, moved, block)
            evp[zz * 2 + cc] = block
    for load in loads[3:]:
        load.wait()

    def place_slots(index, lon_out, hot_out):
        lon = (index * 10923) >> 22
        lat = index - lon * LAT
        lon_out[...] = jnp.broadcast_to(lon, (LEV, SLOTS))
        for n in range(SLOTS // CHUNK):
            rows = lax.broadcasted_iota(jnp.int32, (LAT, CHUNK), 0)
            hot = jnp.where(rows == lat[:, n * CHUNK : (n + 1) * CHUNK], 1.0, 0.0)
            hot_out[:, pl.ds(n * CHUNK, CHUNK)] = hot.astype(BF16)

    live = lax.broadcasted_iota(jnp.int32, (1, SLOTS), 1) < oc[0, 0]
    o0 = jnp.where(live, obs[0], 0.0)
    s1 = o0 / obs[1]
    obs[0] = o0
    obs[2] = s1
    terms[...] = wv[...] * s1
    place_slots(oiv[...], lonb, onehot)

    def pieces(x):
        high = x.astype(BF16)
        return high, (x - high.astype(F32)).astype(BF16)

    def spread(values, lons, hot):
        total = jnp.zeros((LON * LEV, LAT), F32)
        for n in range(SLOTS // CHUNK):
            cols = pl.ds(n * CHUNK, CHUNK)
            ids = lax.broadcasted_iota(jnp.int32, (LON, LEV, CHUNK), 0)
            placed = jnp.where(ids == lons[:, cols][None], values[:, cols][None], 0.0).reshape(LON * LEV, CHUNK)
            for piece in pieces(placed):
                total += lax.dot_general(piece, hot[:, cols], (((1,), (1,)), ((), ())), preferred_element_type=F32)
        return total.reshape(LON, LEV, LAT)

    def observe(field, row):
        high, low = pieces(field.reshape(LON * LEV, LAT))
        for n in range(SLOTS // CHUNK):
            cols = pl.ds(n * CHUNK, CHUNK)
            picked = jnp.dot(high, onehot[:, cols], preferred_element_type=F32)
            picked += jnp.dot(low, onehot[:, cols], preferred_element_type=F32)
            picked = picked.reshape(LON, LEV, CHUNK)
            here = lonb[:, cols]
            column = jnp.zeros((LEV, CHUNK), F32)
            for i in range(LON):
                column = jnp.where(here == i, picked[i], column)
            total = jnp.sum(column * wv[:, cols], axis=0, keepdims=True)
            slot = lax.broadcasted_iota(jnp.int32, (1, CHUNK), 1) + n * CHUNK
            obs[row, :, cols] = jnp.where(slot < oc[0, 0], total, 0.0)

    halo = [
        send(ac.at[:, pl.ds(HALO, HALO)], ac.at[:, pl.ds(HALO + LON, HALO)], sem_hs.at[0], sem_hr.at[0], k, west),
        send(ac.at[:, pl.ds(LON, HALO)], ac.at[:, pl.ds(0, HALO)], sem_hs.at[1], sem_hr.at[1], k, east),
    ]
    loads[1].wait()
    loads[2].wait()
    pl.semaphore_wait(barrier, 34)

    me = zh * 2 + c
    first = []
    for j in FAR_FIRST:
        peer, back = (me + j) % SIDE, (me + SIDE - j) % SIDE
        out = send(evp.at[peer], r1.at[me], sem_1s.at[j], sem_1r.at[j], *on_zc(peer))
        out.start()
        first.append((out, send(evp.at[peer], r1.at[back], sem_1s.at[j], sem_1r.at[j], *on_zc(back))))
    r1[pl.ds(me, 1)] = evp[pl.ds(me, 1)]

    for copy in halo:
        copy.start()

    gsend = [
        send(terms, terms_n, sem_gs.at[0], sem_gr.at[0], before, t),
        send(oiv, oiv_n, sem_gs.at[1], sem_gr.at[1], before, t),
    ]
    for copy in gsend:
        copy.start()

    gb[...] = spread(terms, lonb, onehot)
    for lt in range(LAT // 128):
        sl = pl.ds(lt * 128, 128)
        u = gb[:, :, sl]
        for n, off in ((8, 0), (4, 8), (2, 12), (1, 14)):
            pair = u.reshape(n, 2, LEV, 128)
            hb[pl.ds(off, n), :, sl] = pair[:, 0] - pair[:, 1]
            u = pair[:, 0] + pair[:, 1]
        cu[pl.ds(place, 1), :, sl] = u
    for j in FAR_FIRST:
        kk, tt = on_zx((me_zx + 4 * j) % 32)
        pl.semaphore_signal(sem_in, inc=1, device_id=(kk, tt), device_id_type=MESH)

    coarse = []
    for j in range(1, 4):
        peer, back = (place + j) % 4, (place + 4 - j) % 4
        out = send(cu.at[place], cu.at[place], sem_cs.at[j], sem_cr.at[j], k, base + peer)
        out.start()
        coarse.append((out, send(cu.at[place], cu.at[back], sem_cs.at[j], sem_cr.at[j], k, base + back)))

    level_ids = lax.broadcasted_iota(jnp.int32, (LEV, LEV), 0)
    other_ids = lax.broadcasted_iota(jnp.int32, (LEV, LEV), 1)
    mixing = vmv[0] + jnp.where(level_ids == other_ids, 0.7, 0.0).astype(F32)
    for r in range(LEV):
        chosen = jnp.where(other_ids == (level_ids + r) % LEV, mixing, 0.0)
        mixf[r] = jnp.broadcast_to(jnp.sum(chosen, axis=1, keepdims=True), (LEV, LAT))
    mixb[0] = mixf[0]
    for r in range(1, LEV):
        mixb[r] = pltpu.roll(mixf[LEV - r], LEV - r, 0)
    lanes = lax.broadcasted_iota(jnp.int32, (LEV, LAT), 1)
    dn = jnp.where(lanes < LAT - 1, dfv[0], 0.0)
    dp = pltpu.roll(dn, 1, 1)
    latc[0] = dn
    latc[1] = dp
    latc[2] = 1.0 - dn - dp

    def weigh(start, count):
        cols = pl.ds(start, count)
        c = ac[1, cols]
        sq = c * c
        wts[0, cols] = (sq + c) * 0.5
        wts[1, cols] = 1.0 - sq
        wts[2, cols] = (sq - c) * 0.5

    for n in range(4):
        weigh(HALO + 4 * n, 4)

    def latitude(a):
        return latc[2] * a + latc[0] * pltpu.roll(a, LAT - 1, 2) + latc[1] * pltpu.roll(a, 1, 2)

    def couple(b, mix):
        total = mix[0] * b
        for r in range(1, LEV):
            total += mix[r] * pltpu.roll(b, LEV - r, 1)
        return total

    def forward(start, out):
        path = [(start, bufa, 0), (bufa, bufb, 0), (bufb, bufa, 0), (bufa, out, HALO)]
        for step, ((src, dst, off), blocks) in enumerate(zip(path, (6, 5, 5, 4))):

            def block(n, carry):
                i = step + 1 + 4 * n
                u = src[pl.ds(i - 1, 6)]
                a = wts[0, pl.ds(i, 4)] * u[0:4] + wts[1, pl.ds(i, 4)] * u[1:5] + wts[2, pl.ds(i, 4)] * u[2:6]
                dst[pl.ds(i - off, 4)] = couple(latitude(a), mixf)
                return carry

            lax.fori_loop(0, blocks, block, 0, unroll=True)

    def backward(start, out):
        path = [(start, bufa, 0), (bufa, bufb, 0), (bufb, bufa, 0), (bufa, out, HALO)]
        for step, ((src, dst, off), wide, narrow) in enumerate(zip(path, (6, 6, 5, 5), (6, 5, 5, 4))):

            def inner(n, carry):
                i = step + 4 * n
                bufg[pl.ds(i, 4)] = latitude(couple(src[pl.ds(i, 4)], mixb))
                return carry

            def outer(n, carry):
                i = step + 1 + 4 * n
                z = wts[1, pl.ds(i, 4)] * bufg[pl.ds(i, 4)]
                z += wts[0, pl.ds(i + 1, 4)] * bufg[pl.ds(i + 1, 4)]
                z += wts[2, pl.ds(i - 1, 4)] * bufg[pl.ds(i - 1, 4)]
                dst[pl.ds(i - off, 4)] = z
                return carry

            lax.fori_loop(0, wide, inner, 0, unroll=True)
            lax.fori_loop(0, narrow, outer, 0, unroll=True)

    for copy in halo:
        copy.wait()
    weigh(0, HALO)
    weigh(HALO + LON, HALO)
    forward(ac.at[0], mo.at[0])
    shift = send(mo.at[0], ma, sem_ts.at[0], sem_tr.at[0], later, t)
    asend = send(ac.at[0, pl.ds(HALO, LON)], an, sem_ts.at[1], sem_tr.at[1], before, t)
    shift.start()
    asend.start()

    observe(ac[0, pl.ds(HALO, LON)], 3)
    q1 = obs[0] + obs[3]
    obs[3] = q1
    obs[4] = q1 / obs[1]


    for out, came in first:
        came.wait_recv()
    turned = jnp.transpose(r1[...].reshape(LAT, 128))
    s2[...] = turned.reshape(SIDE, LON, LAT)
    second = []
    for j in FAR_FIRST:
        peer, back = (y + j) % SIDE, (y + SIDE - j) % SIDE
        out = send(s2.at[peer], r2.at[y], sem_2s.at[j], sem_2r.at[j], *on_y(peer))
        out.start()
        second.append((out, send(s2.at[peer], r2.at[back], sem_2s.at[j], sem_2r.at[j], *on_y(back))))
    r2[pl.ds(y, 1)] = s2[pl.ds(y, 1)]

    for copy in gsend:
        copy.wait()
    place_slots(oiv_n[...], lonb_n, onehot_n)
    gx[pl.ds(HALO, LON)] = spread(terms_n, lonb_n, onehot_n)
    gedge = [
        send(gx.at[pl.ds(HALO, HALO)], gx.at[pl.ds(HALO + LON, HALO)], sem_hs.at[4], sem_hr.at[4], k, west),
        send(gx.at[pl.ds(LON, HALO)], gx.at[pl.ds(0, HALO)], sem_hs.at[5], sem_hr.at[5], k, east),
    ]
    for copy in gedge:
        copy.start()

    htq[...] = spread(wv[...] * obs[4], lonb, onehot)

    for out, came in coarse:
        came.wait_recv()
    for out, came in second:
        came.wait_recv()
    lane = lax.broadcasted_iota(jnp.int32, (LON, LAT), 1)
    for zz in range(4):
        for half in range(2):
            level = None
            for m in range(4):
                offset = (96 * (m - zz)) % LAT
                part = r2[half * 4 + m]
                moved = pltpu.roll(part, offset, 1) if offset else part
                level = moved if level is None else jnp.where(lane >= 96 * m, moved, level)
            vt[zz * 2 + half] = level
    vb[...] = jnp.swapaxes(vt[...], 0, 1)
    u = [cu[j] for j in range(4)]
    left, right = jnp.where(place < 2, u[0], u[2]), jnp.where(place < 2, u[1], u[3])
    total = (u[0] + u[1]) + jnp.where(place == 0, u[2] + u[3], -(u[2] + u[3]))
    coefficient = jnp.where(place % 2 == 0, total * (1 / 64), (left - right) * (1 / 32))
    wq[place] = coefficient * vb[0]
    wsend = []
    for j in range(1, 4):
        peer, back = (place + j) % 4, (place + 4 - j) % 4
        out = send(wq.at[place], wq.at[place], sem_ws.at[j], sem_wr.at[j], k, base + peer)
        out.start()
        wsend.append((out, send(wq.at[place], wq.at[back], sem_ws.at[j], sem_wr.at[j], k, base + back)))
    wside = [
        send(wq.at[place], wn.at[place], sem_ws.at[4], sem_wr.at[4 + place], k, (base + TILES - 1) % TILES),
        send(wq.at[place], wn.at[place], sem_ws.at[5], sem_wr.at[4 + place], k, (base + 4) % TILES),
    ]
    for copy in wside:
        copy.start()

    shift.wait()
    for lt in range(LAT // 128):
        sl = pl.ds(lt * 128, 128)
        u = None
        for n, off, half in ((1, 14, 1 / 16), (2, 12, 1 / 8), (4, 8, 1 / 4), (8, 0, 1 / 2)):
            width = LON // n
            var = vb[:, :, sl].reshape(n, width, LEV, 128)[:, width // 2]
            d = hb[pl.ds(off, n), :, sl] * var * half
            u = jnp.concatenate([d, -d]) if u is None else jnp.stack([u + d, u - d], axis=1).reshape(2 * n, LEV, 128)
        dx[pl.ds(HALO, LON), :, sl] = ac[0, pl.ds(HALO, LON), :, sl] - jnp.where(k > 0, ma[:, :, sl], 0.0) - u
    edge = [
        send(dx.at[pl.ds(HALO, HALO)], dx.at[pl.ds(HALO + LON, HALO)], sem_hs.at[2], sem_hr.at[2], k, west),
        send(dx.at[pl.ds(LON, HALO)], dx.at[pl.ds(0, HALO)], sem_hs.at[3], sem_hr.at[3], k, east),
    ]
    for copy in edge:
        copy.start()
    for copy in gedge:
        copy.wait()
    backward(gx, mtg)
    observe(dx[pl.ds(HALO, LON)], 5)

    def state_part(n, acc):
        cols = pl.ds(4 * n, 4)
        g = gb[cols]
        f = g - jnp.where(k < WINDOWS - 1, mtg[cols], 0.0) + htq[cols]
        return acc[0] + jnp.sum(g * g, axis=0), acc[1] + jnp.sum(g * f, axis=0), acc[2] + jnp.sum(f * f, axis=0)

    zero = jnp.zeros((LEV, LAT), F32)
    gg, gf, ff = lax.fori_loop(0, 4, state_part, (zero, zero, zero), unroll=True)
    for out, came in wsend:
        came.wait_recv()

    @pl.when((place == 0) | (place == 3))
    def _():
        for j in range(4):
            send(wq.at[j], wn.at[j], sem_ws.at[4], sem_wr.at[4 + j], k, beside + j).wait_recv()

    for copy in edge:
        copy.wait()

    def on_tile(w, at):
        pair = jnp.where(at < 2, w[0] + w[2], w[0] - w[2])
        fine = jnp.where(at < 2, w[1], w[3])
        return pair + jnp.where(at % 2 == 0, fine, -fine)

    up[0] = jnp.where(place > 0, on_tile(wq, place - 1), on_tile(wn, 3))
    up[1] = on_tile(wq, place)
    up[2] = jnp.where(place < 3, on_tile(wq, place + 1), on_tile(wn, 0))
    for n, start, count in ((0, 0, HALO), (1, HALO, LON), (2, HALO + LON, HALO)):
        dx[pl.ds(start, count)] = dx[pl.ds(start, count)] - up[n][None]
    dd[...] = dx[pl.ds(HALO, LON)]

    def fold(x):
        x = jnp.sum(x, axis=0, keepdims=True)
        return sum(x[:, n : n + 128] for n in range(0, x.shape[1], 128))

    o0, q1 = obs[0], obs[3]
    picked = sum(jnp.dot(piece, onehot[...], preferred_element_type=F32) for piece in pieces(up[1]))
    flat = jnp.sum(picked * wv[...], axis=0, keepdims=True)
    h = q1 + obs[5] - jnp.where(live, flat, 0.0)
    sums = [fold(o0 * q1), fold(gg) + fold(q1 * q1), fold(o0 * h), fold(gf) + fold(q1 * h), fold(ff) + fold(h * h)]
    forward(dx, mo.at[1])

    asend.wait()

    def lam_part(n, acc):
        cols = pl.ds(4 * n, 4)
        a = an[cols]
        b = a - jnp.where(k < WINDOWS - 1, mo[0, cols], 0.0)
        e = b - jnp.where(k < WINDOWS - 1, mo[1, cols], 0.0)
        products = (a * b, b * b, a * e, b * e, e * e)
        return tuple(total + jnp.sum(product, axis=0) for total, product in zip(acc, products))

    acc = lax.fori_loop(0, 4, lam_part, (zero,) * 5, unroll=True)
    row = lax.broadcasted_iota(jnp.int32, (8, 128), 0)
    total = jnp.zeros((8, 128), F32)
    for n in range(5):
        total = jnp.where(row == n, sums[n] + fold(acc[n]), total)
    diagonal = row == lax.broadcasted_iota(jnp.int32, (8, 128), 1)
    total = jnp.sum(total, axis=1, keepdims=True)
    total = jnp.sum(jnp.where(diagonal, total, 0.0), axis=0, keepdims=True)

    for stage, (me, ring, order, arr) in enumerate(((me_yc, on_yc, FAR_YC, arr1), (me_zx, on_zx, FAR_ZX, arr2))):
        count = len(order) + 1
        if stage == 1:
            pl.semaphore_wait(sem_in, SIDE - 1)
        arr[0] = total
        for j in order:
            send(arr.at[0], arr.at[j], sem_a.at[stage, 0], sem_a.at[stage, 1], *ring((me + j) % count)).start()
        others = arr.at[pl.ds(1, count - 1)]
        send(others, others, sem_a.at[stage, 0], sem_a.at[stage, 1], *ring((me + 1) % count)).wait_recv()
        total = jnp.sum(arr[...], axis=0)
    total = jnp.sum(jnp.where(diagonal, total, 0.0), axis=1, keepdims=True)
    rq, qq, re, qe, ee = (total[n : n + 1] for n in range(5))
    alpha = rq / (qq + 1e-6)
    beta = alpha * (1e-6 - re + alpha * qe) / (qq - 2.0 * alpha * qe + alpha * alpha * ee + 1e-6)
    row = lax.broadcasted_iota(jnp.int32, (8, 128), 0)
    al[...] = jnp.where(row == 0, alpha, beta)
    ao[...] = ac[0, pl.ds(HALO, LON)]
    so[0] = obs[2]
    so[1] = obs[4]

    for out, came in first + second + coarse + wsend:
        out.wait_send()
    for copy in wside:
        copy.wait_send()
    for stage, (ring, arr) in enumerate(((on_yc, arr1), (on_zx, arr2))):
        others = arr.at[pl.ds(1, arr.shape[0] - 1)]
        send(others, others, sem_a.at[stage, 0], sem_a.at[stage, 1], *ring(0)).wait_send()


def finish(gb, dd, ao, so, al, mult, omult, incr):
    alpha, beta = al[0:1, 0:1], al[1:2, 0:1]
    both, cross = alpha + beta, alpha * beta
    wide_both, wide_cross = jnp.broadcast_to(both, (LEV, LAT)), jnp.broadcast_to(cross, (LEV, LAT))
    mult[0] = -wide_cross * gb[...]
    incr[0] = wide_both * ao[...] - wide_cross * dd[...]
    omult[...] = both * so[0] - cross * so[1]


def field(*lead):
    return pltpu.VMEM((*lead, LEV, LAT), F32)


SCRATCH = [
    field(2, WIDE),
    field(3, WIDE),
    pltpu.VMEM((LAT, SLOTS), BF16),
    pltpu.VMEM((LAT, SLOTS), BF16),
    pltpu.VMEM((LEV, SLOTS), jnp.int32),
    pltpu.VMEM((LEV, SLOTS), jnp.int32),
    pltpu.VMEM((6, 1, SLOTS), F32),
    pltpu.VMEM((1, SLOTS), jnp.int32),
    pltpu.VMEM((1, SLOTS), jnp.int32),
    pltpu.VMEM((LEV, SLOTS), F32),
    pltpu.VMEM((LEV, SLOTS), F32),
    pltpu.VMEM((LEV, SLOTS), F32),
    field(1),
    pltpu.VMEM((1, LEV, LEV), F32),
    field(3),
    field(LEV),
    field(LEV),
    field(WIDE),
    field(WIDE),
    field(WIDE),
    field(WIDE),
    field(2, LON),
    field(LON),
    field(LON),
    field(LON),
    field(LON),
    field(WIDE),
    field(LON),
    field(4),
    pltpu.VMEM((LAT // SIDE, TILES * LON), F32),
    pltpu.VMEM((SIDE, LAT // SIDE, 128), F32),
    pltpu.VMEM((SIDE, LAT // SIDE, 128), F32),
    pltpu.VMEM((SIDE, LON, LAT), F32),
    pltpu.VMEM((SIDE, LON, LAT), F32),
    pltpu.VMEM((LEV, LON, LAT), F32),
    field(LON),
    field(4),
    field(4),
    field(3),
    pltpu.VMEM((16, 1, 128), F32),
    pltpu.VMEM((32, 1, 128), F32),
] + [
    pltpu.SemaphoreType.DMA(shape)
    for shape in (
        (9,), (6,), (6,), (8,), (8,), (8,), (8,), (8,), (8,), (4,), (4,), (2,), (2,), (2,), (2,), (2, 2),
    )
] + [pltpu.SemaphoreType.REGULAR]


def body(md, od, ov, ow, oi, oc, cr, df, vm, ev):
    inputs = (md[0], od, ov, ow[0], oi, oc, cr[0], df, vm, jnp.swapaxes(ev[0], 0, 1))
    inputs = [x if x is oc else pltpu.with_memory_space_constraint(x, pltpu.HBM) for x in inputs]
    hbm = [pl.BlockSpec(memory_space=pltpu.HBM)]
    vmem = pl.BlockSpec(memory_space=pltpu.VMEM)
    plane = jax.ShapeDtypeStruct((LON, LEV, LAT), F32)
    parts = pl.pallas_call(
        kernel,
        out_shape=(plane, plane, plane, jax.ShapeDtypeStruct((2, 1, SLOTS), F32), jax.ShapeDtypeStruct((8, 128), F32)),
        in_specs=hbm * 5 + [pl.BlockSpec(memory_space=pltpu.SMEM)] + hbm * 4,
        out_specs=(vmem,) * 5,
        scratch_shapes=SCRATCH,
        compiler_params=pltpu.CompilerParams(
            collective_id=0, has_side_effects=True, vmem_limit_bytes=40 * 1024 * 1024
        ),
        name="saddle",
    )(*inputs)
    return pl.pallas_call(
        finish,
        out_shape=(
            jax.ShapeDtypeStruct((1, LON, LEV, LAT), F32),
            jax.ShapeDtypeStruct((1, SLOTS), F32),
            jax.ShapeDtypeStruct((1, LON, LEV, LAT), F32),
        ),
        compiler_params=pltpu.CompilerParams(vmem_limit_bytes=8 * 1024 * 1024),
        name="finish",
    )(*parts)


def solution(mesh):
    in_specs = (
        P("tm", "space", None, None),
        P("tm", "space"),
        P("tm", "space"),
        P("tm", None, "space"),
        P("tm", "space"),
        P("tm", "space"),
        P("tm", "space", None, None),
        P("tm", None, None),
        P("tm", None, None),
        P("tm", None, "space"),
    )
    out_specs = (P("tm", "space", None, None), P("tm", "space"), P("tm", "space", None, None))
    return jax.shard_map(body, mesh=mesh, in_specs=in_specs, out_specs=out_specs, check_vma=False)
```

```python
import jax
import jax.numpy as jnp
from jax import lax
from jax.experimental import pallas as pl
from jax.experimental.pallas import tpu as pltpu
from jax.sharding import PartitionSpec as P

MESH = pl.DeviceIdType.MESH
F32 = jnp.float32
BF16 = jnp.bfloat16
LON, LEV, LAT, SLOTS = 16, 8, 384, 2048
WINDOWS, TILES, SIDE = 8, 64, 8
HALO = 4
WIDE = LON + 2 * HALO + 2
CHUNK = 512
FAR_FIRST = (4, 3, 5, 2, 6, 1, 7)
FAR_YC = (8, 7, 9, 6, 10, 5, 11, 4, 12, 3, 13, 2, 14, 1, 15)
FAR_ZX = tuple(sorted(range(1, 32), key=lambda j: (-min(j // 4, 8 - j // 4), j)))


def kernel(
    md, od, ov, ow, oi, oc, cr, df, vm, ev,
    gb, dd, ao, so, al,
    ac, wts, onehot, onehot_n, lonb, lonb_n, obs, oiv, oiv_n, wv, terms, terms_n, dfv, vmv, latc, mixf, mixb,
    gx, bufa, bufb, bufg, mo, ma, an, mtg, htq, dx,
    hb, cu, evv, evp, r1, s2, r2, vt, vb, wq, wn, up, arr1, arr2,
    sem_load, sem_hs, sem_hr, sem_1s, sem_1r, sem_2s, sem_2r, sem_ws, sem_wr, sem_cs, sem_cr, sem_gs, sem_gr, sem_ts, sem_tr, sem_a, sem_in,
):
    k = lax.axis_index("tm")
    t = lax.axis_index("space")
    x, zl = k // 2, k % 2
    zh, y, c = t // 16, t // 2 % 8, t % 2
    east, west = (t + 1) % TILES, (t + TILES - 1) % TILES
    later, before = (k + 1) % WINDOWS, (k + WINDOWS - 1) % WINDOWS
    place = t % 4
    base = t - place

    def send(src, dst, ssem, rsem, kk, tt):
        return pltpu.make_async_remote_copy(
            src_ref=src, dst_ref=dst, send_sem=ssem, recv_sem=rsem, device_id=(kk, tt), device_id_type=MESH
        )

    def tile_at(zz, yy, cc):
        return zz * 16 + yy * 2 + cc

    def on_y(place):
        return k, tile_at(zh, place, c)

    def on_zc(place):
        return k, tile_at(place // 2, y, place % 2)

    def on_yc(place):
        return k, tile_at(zh, place // 2, place % 2)

    def on_zx(place):
        return place % 4 * 2 + place // 4 % 2, tile_at(place // 8, y, c)

    barrier = pltpu.get_barrier_semaphore()

    def greet(kk, tt):
        pl.semaphore_signal(barrier, inc=1, device_id=(kk, tt), device_id_type=MESH)

    me_yc, me_zx = y * 2 + c, (zh * 2 + zl) * 4 + x
    for j in FAR_YC:
        greet(*on_yc((me_yc + j) % 16))
    for j in FAR_FIRST:
        greet(*on_zx((me_zx + 4 * j) % 32))
    for j in range(1, 4):
        greet(k, tile_at((zh + j) % 4, y, 1 - c))
        greet((x + j) % 4 * 2 + zl, t)
    greet(later, t)
    greet(before, t)
    greet(k, east)
    greet(k, west)
    beside = jnp.where(place == 0, base + TILES - 4, base + 4) % TILES

    @pl.when((place == 0) | (place == 3))
    def _():
        for j in range(4):
            greet(k, beside + j)


    loads = [
        pltpu.make_async_copy(src, dst, sem_load.at[n])
        for n, (src, dst) in enumerate(
            [
                (ev, evv),
                (md, ac.at[0, pl.ds(HALO, LON)]),
                (cr, ac.at[1, pl.ds(HALO, LON)]),
                (oi, oiv),
                (od, obs.at[0]),
                (ov, obs.at[1]),
                (ow, wv),
                (df, dfv),
                (vm, vmv),
            ]
        )
    ]
    for load in loads:
        load.start()

    lane_v = lax.broadcasted_iota(jnp.int32, (LAT // SIDE, 128), 1)
    loads[0].wait()
    for zz in range(4):
        for cc in range(2):
            block = None
            for yy in range(SIDE):
                source = evv[:, pl.ds((zz * 2 + yy // 4) * 128, 128)]
                offset = (yy * 16 - (yy % 4 * 32 + cc * 16)) % 128
                moved = pltpu.roll(source, offset, 1) if offset else source
                block = moved if block is None else jnp.where(lane_v >= yy * 16, moved, block)
            evp[zz * 2 + cc] = block
    for load in loads[3:]:
        load.wait()

    def place_slots(index, lon_out, hot_out):
        lon = (index * 10923) >> 22
        lat = index - lon * LAT
        lon_out[...] = jnp.broadcast_to(lon, (LEV, SLOTS))
        for n in range(SLOTS // CHUNK):
            rows = lax.broadcasted_iota(jnp.int32, (LAT, CHUNK), 0)
            hot = jnp.where(rows == lat[:, n * CHUNK : (n + 1) * CHUNK], 1.0, 0.0)
            hot_out[:, pl.ds(n * CHUNK, CHUNK)] = hot.astype(BF16)

    live = lax.broadcasted_iota(jnp.int32, (1, SLOTS), 1) < oc[0, 0]
    o0 = jnp.where(live, obs[0], 0.0)
    s1 = o0 / obs[1]
    obs[0] = o0
    obs[2] = s1
    terms[...] = wv[...] * s1
    place_slots(oiv[...], lonb, onehot)

    def pieces(x):
        high = x.astype(BF16)
        return high, (x - high.astype(F32)).astype(BF16)

    def spread(values, lons, hot):
        total = jnp.zeros((LON * LEV, LAT), F32)
        for n in range(SLOTS // CHUNK):
            cols = pl.ds(n * CHUNK, CHUNK)
            ids = lax.broadcasted_iota(jnp.int32, (LON, LEV, CHUNK), 0)
            placed = jnp.where(ids == lons[:, cols][None], values[:, cols][None], 0.0).reshape(LON * LEV, CHUNK)
            for piece in pieces(placed):
                total += lax.dot_general(piece, hot[:, cols], (((1,), (1,)), ((), ())), preferred_element_type=F32)
        return total.reshape(LON, LEV, LAT)

    def observe(field, row):
        high, low = pieces(field.reshape(LON * LEV, LAT))
        for n in range(SLOTS // CHUNK):
            cols = pl.ds(n * CHUNK, CHUNK)
            picked = jnp.dot(high, onehot[:, cols], preferred_element_type=F32)
            picked += jnp.dot(low, onehot[:, cols], preferred_element_type=F32)
            picked = picked.reshape(LON, LEV, CHUNK)
            here = lonb[:, cols]
            column = jnp.zeros((LEV, CHUNK), F32)
            for i in range(LON):
                column = jnp.where(here == i, picked[i], column)
            total = jnp.sum(column * wv[:, cols], axis=0, keepdims=True)
            slot = lax.broadcasted_iota(jnp.int32, (1, CHUNK), 1) + n * CHUNK
            obs[row, :, cols] = jnp.where(slot < oc[0, 0], total, 0.0)

    halo = [
        send(ac.at[:, pl.ds(HALO, HALO)], ac.at[:, pl.ds(HALO + LON, HALO)], sem_hs.at[0], sem_hr.at[0], k, west),
        send(ac.at[:, pl.ds(LON, HALO)], ac.at[:, pl.ds(0, HALO)], sem_hs.at[1], sem_hr.at[1], k, east),
    ]
    loads[1].wait()
    loads[2].wait()
    pl.semaphore_wait(barrier, 34)

    me = zh * 2 + c
    first = []
    for j in FAR_FIRST:
        peer, back = (me + j) % SIDE, (me + SIDE - j) % SIDE
        out = send(evp.at[peer], r1.at[me], sem_1s.at[j], sem_1r.at[j], *on_zc(peer))
        out.start()
        first.append((out, send(evp.at[peer], r1.at[back], sem_1s.at[j], sem_1r.at[j], *on_zc(back))))
    r1[pl.ds(me, 1)] = evp[pl.ds(me, 1)]

    for copy in halo:
        copy.start()

    gsend = [
        send(terms, terms_n, sem_gs.at[0], sem_gr.at[0], before, t),
        send(oiv, oiv_n, sem_gs.at[1], sem_gr.at[1], before, t),
    ]
    for copy in gsend:
        copy.start()

    gb[...] = spread(terms, lonb, onehot)
    for lt in range(LAT // 128):
        sl = pl.ds(lt * 128, 128)
        u = gb[:, :, sl]
        for n, off in ((8, 0), (4, 8), (2, 12), (1, 14)):
            pair = u.reshape(n, 2, LEV, 128)
            hb[pl.ds(off, n), :, sl] = pair[:, 0] - pair[:, 1]
            u = pair[:, 0] + pair[:, 1]
        cu[pl.ds(place, 1), :, sl] = u
    for j in FAR_FIRST:
        kk, tt = on_zx((me_zx + 4 * j) % 32)
        pl.semaphore_signal(sem_in, inc=1, device_id=(kk, tt), device_id_type=MESH)

    coarse = []
    for j in range(1, 4):
        peer, back = (place + j) % 4, (place + 4 - j) % 4
        out = send(cu.at[place], cu.at[place], sem_cs.at[j], sem_cr.at[j], k, base + peer)
        out.start()
        coarse.append((out, send(cu.at[place], cu.at[back], sem_cs.at[j], sem_cr.at[j], k, base + back)))

    level_ids = lax.broadcasted_iota(jnp.int32, (LEV, LEV), 0)
    other_ids = lax.broadcasted_iota(jnp.int32, (LEV, LEV), 1)
    mixing = vmv[0] + jnp.where(level_ids == other_ids, 0.7, 0.0).astype(F32)
    for r in range(LEV):
        chosen = jnp.where(other_ids == (level_ids + r) % LEV, mixing, 0.0)
        mixf[r] = jnp.broadcast_to(jnp.sum(chosen, axis=1, keepdims=True), (LEV, LAT))
    mixb[0] = mixf[0]
    for r in range(1, LEV):
        mixb[r] = pltpu.roll(mixf[LEV - r], LEV - r, 0)
    lanes = lax.broadcasted_iota(jnp.int32, (LEV, LAT), 1)
    dn = jnp.where(lanes < LAT - 1, dfv[0], 0.0)
    dp = pltpu.roll(dn, 1, 1)
    latc[0] = dn
    latc[1] = dp
    latc[2] = 1.0 - dn - dp

    def weigh(start, count):
        cols = pl.ds(start, count)
        c = ac[1, cols]
        sq = c * c
        wts[0, cols] = (sq + c) * 0.5
        wts[1, cols] = 1.0 - sq
        wts[2, cols] = (sq - c) * 0.5

    for n in range(4):
        weigh(HALO + 4 * n, 4)

    def latitude(a):
        return latc[2] * a + latc[0] * pltpu.roll(a, LAT - 1, 2) + latc[1] * pltpu.roll(a, 1, 2)

    def couple(b, mix):
        total = mix[0] * b
        for r in range(1, LEV):
            total += mix[r] * pltpu.roll(b, LEV - r, 1)
        return total

    def forward(start, out):
        path = [(start, bufa, 0), (bufa, bufb, 0), (bufb, bufa, 0), (bufa, out, HALO)]
        for step, ((src, dst, off), blocks) in enumerate(zip(path, (6, 5, 5, 4))):

            def block(n, carry):
                i = step + 1 + 4 * n
                u = src[pl.ds(i - 1, 6)]
                a = wts[0, pl.ds(i, 4)] * u[0:4] + wts[1, pl.ds(i, 4)] * u[1:5] + wts[2, pl.ds(i, 4)] * u[2:6]
                dst[pl.ds(i - off, 4)] = couple(latitude(a), mixf)
                return carry

            lax.fori_loop(0, blocks, block, 0, unroll=True)

    def forward_in(start, out, parts):
        path = [(start, bufa, 0), (bufa, bufb, 0), (bufb, bufa, 0), (bufa, out, HALO)]
        for (src, dst, off), blocks in zip(path, parts):
            for i, n in blocks:
                u = src[pl.ds(i - 1, n + 2)]
                a = wts[0, pl.ds(i, n)] * u[0:n] + wts[1, pl.ds(i, n)] * u[1 : n + 1] + wts[2, pl.ds(i, n)] * u[2 : n + 2]
                dst[pl.ds(i - off, n)] = couple(latitude(a), mixf)

    def backward(start, out):
        path = [(start, bufa, 0), (bufa, bufb, 0), (bufb, bufa, 0), (bufa, out, HALO)]
        for step, ((src, dst, off), wide, narrow) in enumerate(zip(path, (6, 6, 5, 5), (6, 5, 5, 4))):

            def inner(n, carry):
                i = step + 4 * n
                bufg[pl.ds(i, 4)] = latitude(couple(src[pl.ds(i, 4)], mixb))
                return carry

            def outer(n, carry):
                i = step + 1 + 4 * n
                z = wts[1, pl.ds(i, 4)] * bufg[pl.ds(i, 4)]
                z += wts[0, pl.ds(i + 1, 4)] * bufg[pl.ds(i + 1, 4)]
                z += wts[2, pl.ds(i - 1, 4)] * bufg[pl.ds(i - 1, 4)]
                dst[pl.ds(i - off, 4)] = z
                return carry

            lax.fori_loop(0, wide, inner, 0, unroll=True)
            lax.fori_loop(0, narrow, outer, 0, unroll=True)

    for copy in halo:
        copy.wait()
    weigh(0, HALO)
    weigh(HALO + LON, HALO)
    forward(ac.at[0], mo.at[0])
    shift = send(mo.at[0], ma, sem_ts.at[0], sem_tr.at[0], later, t)
    asend = send(ac.at[0, pl.ds(HALO, LON)], an, sem_ts.at[1], sem_tr.at[1], before, t)
    shift.start()
    asend.start()

    observe(ac[0, pl.ds(HALO, LON)], 3)
    q1 = obs[0] + obs[3]
    obs[3] = q1
    obs[4] = q1 / obs[1]


    for out, came in first:
        came.wait_recv()
    turned = jnp.transpose(r1[...].reshape(LAT, 128))
    s2[...] = turned.reshape(SIDE, LON, LAT)
    second = []
    for j in FAR_FIRST:
        peer, back = (y + j) % SIDE, (y + SIDE - j) % SIDE
        out = send(s2.at[peer], r2.at[y], sem_2s.at[j], sem_2r.at[j], *on_y(peer))
        out.start()
        second.append((out, send(s2.at[peer], r2.at[back], sem_2s.at[j], sem_2r.at[j], *on_y(back))))
    r2[pl.ds(y, 1)] = s2[pl.ds(y, 1)]

    for copy in gsend:
        copy.wait()
    place_slots(oiv_n[...], lonb_n, onehot_n)
    gx[pl.ds(HALO, LON)] = spread(terms_n, lonb_n, onehot_n)
    gedge = [
        send(gx.at[pl.ds(HALO, HALO)], gx.at[pl.ds(HALO + LON, HALO)], sem_hs.at[4], sem_hr.at[4], k, west),
        send(gx.at[pl.ds(LON, HALO)], gx.at[pl.ds(0, HALO)], sem_hs.at[5], sem_hr.at[5], k, east),
    ]
    for copy in gedge:
        copy.start()

    htq[...] = spread(wv[...] * obs[4], lonb, onehot)

    for out, came in coarse:
        came.wait_recv()
    for out, came in second:
        came.wait_recv()
    lane = lax.broadcasted_iota(jnp.int32, (LON, LAT), 1)
    for zz in range(4):
        for half in range(2):
            level = None
            for m in range(4):
                offset = (96 * (m - zz)) % LAT
                part = r2[half * 4 + m]
                moved = pltpu.roll(part, offset, 1) if offset else part
                level = moved if level is None else jnp.where(lane >= 96 * m, moved, level)
            vt[zz * 2 + half] = level
    vb[...] = jnp.swapaxes(vt[...], 0, 1)
    u = [cu[j] for j in range(4)]
    left, right = jnp.where(place < 2, u[0], u[2]), jnp.where(place < 2, u[1], u[3])
    total = (u[0] + u[1]) + jnp.where(place == 0, u[2] + u[3], -(u[2] + u[3]))
    coefficient = jnp.where(place % 2 == 0, total * (1 / 64), (left - right) * (1 / 32))
    wq[place] = coefficient * vb[0]
    wsend = []
    for j in range(1, 4):
        peer, back = (place + j) % 4, (place + 4 - j) % 4
        out = send(wq.at[place], wq.at[place], sem_ws.at[j], sem_wr.at[j], k, base + peer)
        out.start()
        wsend.append((out, send(wq.at[place], wq.at[back], sem_ws.at[j], sem_wr.at[j], k, base + back)))
    wside = [
        send(wq.at[place], wn.at[place], sem_ws.at[4], sem_wr.at[4 + place], k, (base + TILES - 1) % TILES),
        send(wq.at[place], wn.at[place], sem_ws.at[5], sem_wr.at[4 + place], k, (base + 4) % TILES),
    ]
    for copy in wside:
        copy.start()

    ao[...] = ac[0, pl.ds(HALO, LON)]
    so[0] = obs[2]
    so[1] = obs[4]
    shift.wait()
    for lt in range(LAT // 128):
        sl = pl.ds(lt * 128, 128)
        u = None
        for n, off, half in ((1, 14, 1 / 16), (2, 12, 1 / 8), (4, 8, 1 / 4), (8, 0, 1 / 2)):
            width = LON // n
            var = vb[:, :, sl].reshape(n, width, LEV, 128)[:, width // 2]
            d = hb[pl.ds(off, n), :, sl] * var * half
            u = jnp.concatenate([d, -d]) if u is None else jnp.stack([u + d, u - d], axis=1).reshape(2 * n, LEV, 128)
        dx[pl.ds(HALO, LON), :, sl] = ac[0, pl.ds(HALO, LON), :, sl] - jnp.where(k > 0, ma[:, :, sl], 0.0) - u
    edge = [
        send(dx.at[pl.ds(HALO, HALO)], dx.at[pl.ds(HALO + LON, HALO)], sem_hs.at[2], sem_hr.at[2], k, west),
        send(dx.at[pl.ds(LON, HALO)], dx.at[pl.ds(0, HALO)], sem_hs.at[3], sem_hr.at[3], k, east),
    ]
    for copy in edge:
        copy.start()
    observe(dx[pl.ds(HALO, LON)], 5)
    for copy in gedge:
        copy.wait()
    backward(gx, mtg)

    def state_part(n, acc):
        cols = pl.ds(4 * n, 4)
        g = gb[cols]
        f = g - jnp.where(k < WINDOWS - 1, mtg[cols], 0.0) + htq[cols]
        return acc[0] + jnp.sum(g * g, axis=0), acc[1] + jnp.sum(g * f, axis=0), acc[2] + jnp.sum(f * f, axis=0)

    zero = jnp.zeros((LEV, LAT), F32)
    gg, gf, ff = lax.fori_loop(0, 4, state_part, (zero, zero, zero), unroll=True)
    for out, came in wsend:
        came.wait_recv()

    def on_tile(w, at):
        pair = jnp.where(at < 2, w[0] + w[2], w[0] - w[2])
        fine = jnp.where(at < 2, w[1], w[3])
        return pair + jnp.where(at % 2 == 0, fine, -fine)

    up[1] = on_tile(wq, place)
    for copy in edge:
        copy.wait_send()
    dx[pl.ds(HALO, LON)] = dx[pl.ds(HALO, LON)] - up[1][None]
    dd[...] = dx[pl.ds(HALO, LON)]

    def fold(x):
        x = jnp.sum(x, axis=0, keepdims=True)
        return sum(x[:, n : n + 128] for n in range(0, x.shape[1], 128))

    o0, q1 = obs[0], obs[3]
    picked = sum(jnp.dot(piece, onehot[...], preferred_element_type=F32) for piece in pieces(up[1]))
    flat = jnp.sum(picked * wv[...], axis=0, keepdims=True)
    h = q1 + obs[5] - jnp.where(live, flat, 0.0)
    sums = [fold(o0 * q1), fold(gg) + fold(q1 * q1), fold(o0 * h), fold(gf) + fold(q1 * h), fold(ff) + fold(h * h)]
    inner = [[(i, min(4, 19 - step - i)) for i in range(5 + step, 19 - step, 4)] for step in range(4)]
    forward_in(dx, mo.at[1], inner)
    for copy in edge:
        copy.wait_recv()

    @pl.when((place == 0) | (place == 3))
    def _():
        for j in range(4):
            send(wq.at[j], wn.at[j], sem_ws.at[4], sem_wr.at[4 + j], k, beside + j).wait_recv()

    up[0] = jnp.where(place > 0, on_tile(wq, place - 1), on_tile(wn, 3))
    up[2] = jnp.where(place < 3, on_tile(wq, place + 1), on_tile(wn, 0))
    for n, start in ((0, 0), (2, HALO + LON)):
        dx[pl.ds(start, HALO)] = dx[pl.ds(start, HALO)] - up[n][None]
    forward_in(dx, mo.at[1], [[(1 + step, 4), (19 - step, 4)] for step in range(4)])
    asend.wait()

    def lam_part(n, acc):
        cols = pl.ds(4 * n, 4)
        a = an[cols]
        b = a - jnp.where(k < WINDOWS - 1, mo[0, cols], 0.0)
        e = b - jnp.where(k < WINDOWS - 1, mo[1, cols], 0.0)
        products = (a * b, b * b, a * e, b * e, e * e)
        return tuple(total + jnp.sum(product, axis=0) for total, product in zip(acc, products))

    acc = lax.fori_loop(0, 4, lam_part, (zero,) * 5, unroll=True)
    row = lax.broadcasted_iota(jnp.int32, (8, 128), 0)
    total = jnp.zeros((8, 128), F32)
    for n in range(5):
        total = jnp.where(row == n, sums[n] + fold(acc[n]), total)
    diagonal = row == lax.broadcasted_iota(jnp.int32, (8, 128), 1)
    total = jnp.sum(total, axis=1, keepdims=True)
    total = jnp.sum(jnp.where(diagonal, total, 0.0), axis=0, keepdims=True)

    for stage, (me, ring, order, arr) in enumerate(((me_yc, on_yc, FAR_YC, arr1), (me_zx, on_zx, FAR_ZX, arr2))):
        count = len(order) + 1
        if stage == 1:
            pl.semaphore_wait(sem_in, SIDE - 1)
        arr[0] = total
        for j in order:
            send(arr.at[0], arr.at[j], sem_a.at[stage, 0], sem_a.at[stage, 1], *ring((me + j) % count)).start()
        others = arr.at[pl.ds(1, count - 1)]
        send(others, others, sem_a.at[stage, 0], sem_a.at[stage, 1], *ring((me + 1) % count)).wait_recv()
        total = jnp.sum(arr[...], axis=0)
    total = jnp.sum(jnp.where(diagonal, total, 0.0), axis=1, keepdims=True)
    rq, qq, re, qe, ee = (total[n : n + 1] for n in range(5))
    alpha = rq / (qq + 1e-6)
    beta = alpha * (1e-6 - re + alpha * qe) / (qq - 2.0 * alpha * qe + alpha * alpha * ee + 1e-6)
    row = lax.broadcasted_iota(jnp.int32, (8, 128), 0)
    al[...] = jnp.where(row == 0, alpha, beta)

    for out, came in first + second + coarse + wsend:
        out.wait_send()
    for copy in wside:
        copy.wait_send()
    for stage, (ring, arr) in enumerate(((on_yc, arr1), (on_zx, arr2))):
        others = arr.at[pl.ds(1, arr.shape[0] - 1)]
        send(others, others, sem_a.at[stage, 0], sem_a.at[stage, 1], *ring(0)).wait_send()


def finish(gb, dd, ao, so, al, mult, omult, incr):
    alpha, beta = al[0:1, 0:1], al[1:2, 0:1]
    both, cross = alpha + beta, alpha * beta
    wide_both, wide_cross = jnp.broadcast_to(both, (LEV, LAT)), jnp.broadcast_to(cross, (LEV, LAT))
    mult[0] = -wide_cross * gb[...]
    incr[0] = wide_both * ao[...] - wide_cross * dd[...]
    omult[...] = both * so[0] - cross * so[1]


def field(*lead):
    return pltpu.VMEM((*lead, LEV, LAT), F32)


SCRATCH = [
    field(2, WIDE),
    field(3, WIDE),
    pltpu.VMEM((LAT, SLOTS), BF16),
    pltpu.VMEM((LAT, SLOTS), BF16),
    pltpu.VMEM((LEV, SLOTS), jnp.int32),
    pltpu.VMEM((LEV, SLOTS), jnp.int32),
    pltpu.VMEM((6, 1, SLOTS), F32),
    pltpu.VMEM((1, SLOTS), jnp.int32),
    pltpu.VMEM((1, SLOTS), jnp.int32),
    pltpu.VMEM((LEV, SLOTS), F32),
    pltpu.VMEM((LEV, SLOTS), F32),
    pltpu.VMEM((LEV, SLOTS), F32),
    field(1),
    pltpu.VMEM((1, LEV, LEV), F32),
    field(3),
    field(LEV),
    field(LEV),
    field(WIDE),
    field(WIDE),
    field(WIDE),
    field(WIDE),
    field(2, LON),
    field(LON),
    field(LON),
    field(LON),
    field(LON),
    field(WIDE),
    field(LON),
    field(4),
    pltpu.VMEM((LAT // SIDE, TILES * LON), F32),
    pltpu.VMEM((SIDE, LAT // SIDE, 128), F32),
    pltpu.VMEM((SIDE, LAT // SIDE, 128), F32),
    pltpu.VMEM((SIDE, LON, LAT), F32),
    pltpu.VMEM((SIDE, LON, LAT), F32),
    pltpu.VMEM((LEV, LON, LAT), F32),
    field(LON),
    field(4),
    field(4),
    field(3),
    pltpu.VMEM((16, 1, 128), F32),
    pltpu.VMEM((32, 1, 128), F32),
] + [
    pltpu.SemaphoreType.DMA(shape)
    for shape in (
        (9,), (6,), (6,), (8,), (8,), (8,), (8,), (8,), (8,), (4,), (4,), (2,), (2,), (2,), (2,), (2, 2),
    )
] + [pltpu.SemaphoreType.REGULAR]


def body(md, od, ov, ow, oi, oc, cr, df, vm, ev):
    inputs = (md[0], od, ov, ow[0], oi, oc, cr[0], df, vm, jnp.swapaxes(ev[0], 0, 1))
    inputs = [x if x is oc else pltpu.with_memory_space_constraint(x, pltpu.HBM) for x in inputs]
    hbm = [pl.BlockSpec(memory_space=pltpu.HBM)]
    vmem = pl.BlockSpec(memory_space=pltpu.VMEM)
    plane = jax.ShapeDtypeStruct((LON, LEV, LAT), F32)
    parts = pl.pallas_call(
        kernel,
        out_shape=(plane, plane, plane, jax.ShapeDtypeStruct((2, 1, SLOTS), F32), jax.ShapeDtypeStruct((8, 128), F32)),
        in_specs=hbm * 5 + [pl.BlockSpec(memory_space=pltpu.SMEM)] + hbm * 4,
        out_specs=(vmem,) * 5,
        scratch_shapes=SCRATCH,
        compiler_params=pltpu.CompilerParams(
            collective_id=0, has_side_effects=True, vmem_limit_bytes=40 * 1024 * 1024
        ),
        name="saddle",
    )(*inputs)
    return pl.pallas_call(
        finish,
        out_shape=(
            jax.ShapeDtypeStruct((1, LON, LEV, LAT), F32),
            jax.ShapeDtypeStruct((1, SLOTS), F32),
            jax.ShapeDtypeStruct((1, LON, LEV, LAT), F32),
        ),
        compiler_params=pltpu.CompilerParams(vmem_limit_bytes=8 * 1024 * 1024),
        name="finish",
    )(*parts)


def solution(mesh):
    in_specs = (
        P("tm", "space", None, None),
        P("tm", "space"),
        P("tm", "space"),
        P("tm", None, "space"),
        P("tm", "space"),
        P("tm", "space"),
        P("tm", "space", None, None),
        P("tm", None, None),
        P("tm", None, None),
        P("tm", None, "space"),
    )
    out_specs = (P("tm", "space", None, None), P("tm", "space"), P("tm", "space", None, None))
    return jax.shard_map(body, mesh=mesh, in_specs=in_specs, out_specs=out_specs, check_vma=False)
```
